32 devices in a mesh: px: 4 (over y, core), py: 8 (over z, x).
Axes of the slice: x: 2, y: 2, z: 4, core: 2. Of those that a mesh axis runs over, the one named last changes fastest.
Arguments:
- source: float32 [128, 128, 256], P('px', 'py'), may hold values from -3.5 to 3.7
- density: float32 [128, 128, 256], P('px', 'py'), may hold values from 0.25 to 4
Outputs:
- pressure: float32 [128, 128, 256], P('px', 'py')
The draws below stay inside these ranges and needn't reach their ends.
All inputs are finite; a program needn't handle non-finite values.
Results may differ from the reference program's by a relative error of at most 0.0001.
Values sent between devices are 32-bit elements; how exact they have to be, the bound alone decides.
A program may use at most 128 MiB of HBM per device.

```python
import math
import jax
import jax.numpy as jnp
from jax import lax

LEVELS = 4
COARSE = 8
NX = 128
NY = 128
NZ = 256


def draw_source(key, part):
    subkeys = jax.random.split(jax.random.fold_in(key, 11), 3)
    periods = jax.random.uniform(subkeys[0], (3,), jnp.float32, 40.0, 72.0)
    phases = jax.random.uniform(subkeys[1], (3,), jnp.float32, 0.0, 2.0 * math.pi)
    row_pos = jnp.arange(NX, dtype=jnp.float32)[:, None, None]
    col_pos = jnp.arange(NY, dtype=jnp.float32)[None, :, None]
    plane_pos = jnp.arange(NZ, dtype=jnp.float32)[None, None, :]
    waves = jnp.sin(2.0 * math.pi * row_pos / periods[0] + phases[0]) + jnp.sin(2.0 * math.pi * col_pos / periods[1] + phases[1]) + jnp.sin(2.0 * math.pi * plane_pos / periods[2] + phases[2])
    rough_part = jnp.clip(jax.random.normal(subkeys[2], (NX, NY, NZ), jnp.float32), -3.5, 3.5)
    smooth_part = 0.08 * (1.0 + 0.3 * waves)
    return (rough_part + smooth_part).astype(jnp.float32)


def block_scale(own_key, shape, pieces, low, top_value):
    def one(position, blocks):
        steps = jax.random.uniform(jax.random.fold_in(jax.random.fold_in(own_key, 6), position), (blocks,), jnp.float32, low / len(pieces), top_value / len(pieces))
        return jnp.repeat(jnp.exp(steps), shape[position] // blocks).reshape((-1,) + (1,) * (len(shape) - position - 1))

    loudness = one(*pieces[0])
    for cut in pieces[1:]:
        loudness = loudness * one(*cut)
    return loudness


def setup_inputs(seed: int = 0) -> dict:
    key_of = jax.random.split(jax.random.key(seed), 3)
    return {
        "source": draw_source(jax.random.fold_in(key_of[2], 71), 0),
        "density": jnp.clip(jnp.exp(math.log(4.0) - 2.7725887 * jax.random.uniform(key_of[1], (NX, NY, NZ), jnp.float32) ** block_scale(key_of[1], (NX, NY, NZ), ((0, 4), (1, 8)), -0.2, 0.2)), 0.25, 4.0),
    }


RELAXATION = 0.8


def operate(field_pad, mobility_pad, factor):
    full_pad = jnp.pad(field_pad, ((0, 0), (0, 0), (1, 1)))
    along_x = full_pad[:, 1:-1, 1:-1]
    mob_x = mobility_pad[:, 1:-1, 1:-1]
    flux_x = 0.5 * (mob_x[:-1] + mob_x[1:]) * (along_x[:-1] - along_x[1:])
    summed = flux_x[1:] - flux_x[:-1]
    along_y = full_pad[1:-1, :, 1:-1]
    mob_y = mobility_pad[1:-1, :, 1:-1]
    flux_y = 0.5 * (mob_y[:, :-1] + mob_y[:, 1:]) * (along_y[:, :-1] - along_y[:, 1:])
    summed = summed + (flux_y[:, 1:] - flux_y[:, :-1])
    along_z = full_pad[1:-1, 1:-1, :]
    mob_z = mobility_pad[1:-1, 1:-1, :]
    flux_z = 0.5 * (mob_z[:, :, :-1] + mob_z[:, :, 1:]) * (along_z[:, :, :-1] - along_z[:, :, 1:])
    summed = summed + (flux_z[:, :, 1:] - flux_z[:, :, :-1])
    return factor * summed


def diagonal(mobility_pad, factor):
    centre_mobility = mobility_pad[1:-1, 1:-1, 1:-1]
    summed = 3.0 * centre_mobility
    summed = summed + 0.5 * (mobility_pad[:-2, 1:-1, 1:-1] + mobility_pad[2:, 1:-1, 1:-1])
    summed = summed + 0.5 * (mobility_pad[1:-1, :-2, 1:-1] + mobility_pad[1:-1, 2:, 1:-1])
    summed = summed + 0.5 * (mobility_pad[1:-1, 1:-1, :-2] + mobility_pad[1:-1, 1:-1, 2:])
    return factor * summed


def restrict(values):
    return jnp.mean(values.reshape(values.shape[0] // 2, 2, values.shape[1] // 2, 2, values.shape[2] // 2, 2), axis=(1, 3, 5))


def prolong(values):
    expanded = jnp.broadcast_to(values[:, None, :, None, :, None],
                                (values.shape[0], 2, values.shape[1], 2, values.shape[2], 2))
    return expanded.reshape(values.shape[0] * 2, values.shape[1] * 2, values.shape[2] * 2)


def jacobi_sweep(values, rhs_value, mobility_pad, inverse, factor):
    field_pad = jnp.pad(values, ((1, 1), (1, 1), (0, 0)))
    return values + RELAXATION * (rhs_value - operate(field_pad, mobility_pad, factor)) * inverse


def reference(source, density):
    mobilities = [1.0 / density]
    for level_index in range(1, LEVELS):
        mobilities.append(restrict(mobilities[-1]))
    pads = [jnp.pad(mobility, 1, mode="edge") for mobility in mobilities]
    factors = [0.25 ** level_index for level_index in range(LEVELS)]
    inverses = [1.0 / diagonal(padded, factor) for padded, factor in zip(pads, factors)]
    sources = []
    smoothed = []
    rhs_value = source
    for level_index in range(LEVELS - 1):
        values = jnp.zeros(rhs_value.shape, rhs_value.dtype)
        for sweep_index in range(2):
            values = jacobi_sweep(values, rhs_value, pads[level_index], inverses[level_index], factors[level_index])
        residual = rhs_value - operate(jnp.pad(values, ((1, 1), (1, 1), (0, 0))), pads[level_index], factors[level_index])
        sources.append(rhs_value)
        smoothed.append(values)
        rhs_value = restrict(residual)
    coarse_pad = pads[LEVELS - 1]
    coarse_inverse = inverses[LEVELS - 1]
    coarse_factor = factors[LEVELS - 1]

    def coarse_step(sweep_index, values):
        return jacobi_sweep(values, rhs_value, coarse_pad, coarse_inverse, coarse_factor)

    values = lax.fori_loop(0, COARSE, coarse_step, jnp.zeros(rhs_value.shape, rhs_value.dtype))
    for level_index in reversed(range(LEVELS - 1)):
        values = smoothed[level_index] + prolong(values)
        for sweep_index in range(2):
            values = jacobi_sweep(values, sources[level_index], pads[level_index], inverses[level_index], factors[level_index])
    return values
```

```python
import functools

import jax
import jax.numpy as jnp
from jax import lax
from jax.experimental import pallas as pl
from jax.experimental.pallas import tpu as pltpu
from jax.sharding import PartitionSpec as P

COARSE = 8
LANES = 128
HX0, HY0, HX1, PAD2 = 4, 4, 6, 3
ROWS = 8
DIRECTIONS = [(dx, dy) for dx in (-1, 0, 1) for dy in (-1, 0, 1) if (dx, dy) != (0, 0)]
MESH = pl.DeviceIdType.MESH


def iota(shape, dim):
    return lax.broadcasted_iota(jnp.int32, shape, dim)


def dot(a, b):
    return jnp.dot(a, b, precision=lax.Precision.HIGHEST, preferred_element_type=jnp.float32)


def matrix(shape, test, value):
    return jnp.where(test(iota(shape, 0), iota(shape, 1)), value, 0.0).astype(jnp.float32)


def loop(low, high, body, unroll=1):
    def step(i, carry):
        body(i)
        return carry

    lax.fori_loop(low, high, step, 0, unroll=unroll)


class Level:
    def __init__(self, refs, factor, start, total, rows, lanes, span, packed):
        (self.m, self.wx, self.wy, self.wz, self.k, self.g, self.u) = refs
        self.low, self.high = span
        self.half = 0.5 * factor
        self.start, self.total = start, total
        shape = self.m.shape[1:]
        self.shape, self.packed = shape, packed
        row, lane = iota(shape, 0), iota(shape, 1)
        first, total_y = rows
        nz, stride = lanes
        group = lane // stride if packed else 0
        gy = first + row + group * shape[0]
        gz = lane % stride if packed else lane
        self.row = row

        def keep(pos, count, span):
            plus = (pos != count - 1) & (pos != -1) & (pos != span - 1)
            minus = (pos != 0) & (pos != count)
            return jnp.where(plus, 1.0, 0.0), jnp.where(minus, 1.0, 0.0)

        self.kyp, self.kym = keep(gy, total_y, -9)
        self.kzp, self.kzm = keep(gz, nz, stride)
        self.gz, self.nz = gz, nz

    def y_minus(self, t):
        r = pltpu.roll(t, 1, 0)
        if self.packed:
            r = jnp.where(self.row == 0, pltpu.roll(r, LANES // 2, 1), r)
        return r

    def y_plus(self, t):
        r = pltpu.roll(t, self.shape[0] - 1, 0)
        if self.packed:
            r = jnp.where(self.row == self.shape[0] - 1, pltpu.roll(r, LANES // 2, 1), r)
        return r

    def z_minus(self, t):
        return pltpu.roll(t, 1, 1)

    def z_plus(self, t):
        return pltpu.roll(t, self.shape[1] - 1, 1)

    def clear(self, *refs):
        for i in (self.low - 1, self.high):
            for ref in refs:
                ref[i] = jnp.zeros(self.shape, jnp.float32)

    def face(self, x):
        gx = self.start + x
        return jnp.where((gx != self.total - 1) & (gx != -1), 1.0, 0.0)

    def setup(self):
        before = self.low - 1
        self.wx[before] = (self.half * self.face(before)) * (self.m[before] + self.m[self.low])
        known = self.kyp + self.kym + self.kzp + self.kzm

        def body(x):
            m = self.m[x]
            kxp, kxm = self.face(x), self.face(x - 1)
            wxp = kxp * (m + self.m[x + 1])
            wxm = kxm * (m + self.m[x - 1])
            wyp = self.kyp * (m + self.y_plus(m))
            wym = self.kym * (m + self.y_minus(m))
            wzp = self.kzp * (m + self.z_plus(m))
            wzm = self.kzm * (m + self.z_minus(m))
            missing = 6.0 - (kxp + kxm) - known
            diag = ((wxp + wxm) + (wyp + wym)) + ((wzp + wzm) + 2.0 * m * missing)
            self.wx[x] = self.half * wxp
            self.wy[x] = self.half * wyp
            self.wz[x] = self.half * wzp
            self.k[x] = 0.8 / (self.half * diag)

        loop(self.low, self.high, body)

    def change(self, ref, x):
        v = ref[x]
        wy, wz = self.wy[x], self.wz[x]
        total = self.wx[x] * ref[x + 1] + self.wx[x - 1] * ref[x - 1]
        total = total + (wy * self.y_plus(v) + self.y_minus(wy * v))
        total = total + (wz * self.z_plus(v) + self.z_minus(wz * v))
        return v, self.g[x] + self.k[x] * total

    def sweep(self, src, dst):
        def body(x):
            v, rest = self.change(src, x)
            dst[x] = 0.2 * v + rest

        loop(self.low, self.high, body, 2)

    def residual(self, x):
        v, rest = self.change(self.u, x)
        return (rest - 0.8 * v) / self.k[x]


def columns(width):
    return [slice(c, c + LANES) for c in range(0, width, LANES)]


def pair_rows(tmp, value, count):
    rows, width = value.shape
    parts = []
    for i, c in enumerate(columns(width)):
        tmp[i, 0:rows] = value[:, c]
        parts.append(tmp[i, pl.ds(0, count, stride=2)] + tmp[i, pl.ds(1, count, stride=2)])
    return parts[0] if len(parts) == 1 else jnp.concatenate(parts, 1)


def double_rows(tmp, value):
    rows, width = value.shape
    parts = []
    for i, c in enumerate(columns(width)):
        tmp[i, pl.ds(0, rows, stride=2)] = value[:, c]
        tmp[i, pl.ds(1, rows, stride=2)] = value[:, c]
        parts.append(tmp[i, 0 : 2 * rows])
    return parts[0] if len(parts) == 1 else jnp.concatenate(parts, 1)


def kernel(sizes, source, density, out, den, src, l0, l1, l2, l3, pe0, pe1, pe2, t0, t1, t2,
           tmp, gm, gf, copy_sem, s0, r0, s1, r1, sa, ra, sb, rb):
    px_count, py_count = sizes
    px, py = lax.axis_index("px"), lax.axis_index("py")
    bx, by, nz = source.shape
    nx, ny = bx * px_count, by * py_count
    bx1, by1, bx2, by2 = bx // 2, by // 2, bx // 4, by // 4

    def inside(dx, dy):
        test = None
        for d, pos, count in ((dx, px, px_count), (dy, py, py_count)):
            if d:
                one = (pos < count - 1) if d > 0 else (pos > 0)
                test = one if test is None else test & one
        return test

    def fill(ref, hx, value):
        wide, rows = ref.shape[0], ref.shape[1]

        @pl.when(px == 0)
        def _():
            ref[0:hx] = jnp.full((hx,) + ref.shape[1:], value, jnp.float32)

        @pl.when(px == px_count - 1)
        def _():
            ref[wide - hx :] = jnp.full((hx,) + ref.shape[1:], value, jnp.float32)

        @pl.when(py == 0)
        def _():
            ref[:, 0:ROWS] = jnp.full((wide, ROWS, ref.shape[2]), value, jnp.float32)

        @pl.when(py == py_count - 1)
        def _():
            ref[:, rows - ROWS :] = jnp.full((wide, ROWS, ref.shape[2]), value, jnp.float32)

    def halo(src_ref, offset, dst_ref, hx, block, send, recv, base):
        def part(d, own, count, width, at):
            if d == 0:
                return pl.ds(at, count), pl.ds(width, count)
            if d > 0:
                return pl.ds(at + count - width, width), pl.ds(0, width)
            return pl.ds(at, width), pl.ds(width + count, width)

        def copies(n, dx, dy):
            sx, tx = part(dx, None, block[0], hx, offset[0])
            sy, ty = part(dy, None, block[1], ROWS, offset[1])
            return pltpu.make_async_remote_copy(
                src_ref=src_ref.at[sx, sy],
                dst_ref=dst_ref.at[tx, ty],
                send_sem=send.at[base + n],
                recv_sem=recv.at[base + n],
                device_id=(px + dx, py + dy),
                device_id_type=MESH,
            )

        def start():
            for n, (dx, dy) in enumerate(DIRECTIONS):
                @pl.when(inside(dx, dy))
                def _():
                    copies(n, dx, dy).start()

        def arrive():
            for n, (dx, dy) in enumerate(DIRECTIONS):
                @pl.when(inside(-dx, -dy))
                def _():
                    copies(n, dx, dy).wait_recv()

        def sent():
            for n, (dx, dy) in enumerate(DIRECTIONS):
                @pl.when(inside(dx, dy))
                def _():
                    copies(n, dx, dy).wait_send()

        return start, arrive, sent

    def along(axis, ref, send, recv, base):
        count, me = (py_count, py) if axis else (px_count, px)
        region = ref.at[px, py] if axis else ref.at[px]

        def each(act):
            for k in range(1, count):
                to = lax.rem(me + k, count)
                act(pltpu.make_async_remote_copy(
                    src_ref=region,
                    dst_ref=region,
                    send_sem=send.at[base + k - 1],
                    recv_sem=recv.at[base + k - 1],
                    device_id=(px, to) if axis else (to, py),
                    device_id_type=MESH,
                ))

        def arrive():
            for k in range(1, count):
                frm = lax.rem(me + count - k, count)
                landed = ref.at[px, frm] if axis else ref.at[frm]
                pltpu.make_async_remote_copy(
                    src_ref=landed,
                    dst_ref=landed,
                    send_sem=send.at[base + k - 1],
                    recv_sem=recv.at[base + k - 1],
                    device_id=(px, frm) if axis else (frm, py),
                    device_id_type=MESH,
                ).wait_recv()

        return (lambda: each(lambda c: c.start())), arrive, (lambda: each(lambda c: c.wait_send()))

    m1, f1 = l1[0], l1[5]
    own_copies = [
        pltpu.make_async_copy(a, b.at[pl.ds(HX0, bx), pl.ds(ROWS, by)], copy_sem.at[i])
        for i, (a, b) in enumerate(((density, den), (source, src)))
    ]
    for c in own_copies:
        c.start()
    fill(m1, HX1, 1.0)
    fill(f1, HX1, 0.0)
    fill(den, HX0, 1.0)
    fill(src, HX0, 0.0)

    barrier = pltpu.get_barrier_semaphore()
    for k in range(1, py_count):
        pl.semaphore_signal(barrier, 1, device_id=(px, lax.rem(py + k, py_count)), device_id_type=MESH)
    for k in range(1, px_count):
        pl.semaphore_signal(barrier, 1, device_id=(lax.rem(px + k, px_count), py), device_id_type=MESH)
    for dx, dy in DIRECTIONS:
        if dx and dy:
            @pl.when(inside(dx, dy))
            def _():
                pl.semaphore_signal(barrier, 1, device_id=(px + dx, py + dy), device_id_type=MESH)
    beside_x = jnp.minimum(px, 1) + jnp.minimum(px_count - 1 - px, 1)
    beside_y = jnp.minimum(py, 1) + jnp.minimum(py_count - 1 - py, 1)
    pl.semaphore_wait(barrier, px_count + py_count - 2 + beside_x * beside_y)

    den_start, den_arrive, den_sent = halo(density, (0, 0), den, HX0, (bx, by), s0, r0, 0)
    src_start, src_arrive, src_sent = halo(source, (0, 0), src, HX0, (bx, by), s0, r0, 8)
    den_start()
    src_start()

    r_fine = matrix((nz, LANES), lambda z, c: z // 2 == c, 0.125)
    r_low = matrix((LANES, LANES), lambda z, c: z // 2 == c, 0.125)
    r_high = matrix((LANES, LANES), lambda z, c: z // 2 + LANES // 2 == c, 0.125)
    half = LANES // 2
    r_pack = matrix(
        (LANES, LANES), lambda z, c: (z // half == c // half) & ((z % half) // 2 == c % half), 0.125
    )

    def own_mobility(i):
        a = 1.0 / den[HX0 + 2 * i, ROWS : ROWS + by]
        b = 1.0 / den[HX0 + 2 * i + 1, ROWS : ROWS + by]
        t0[i] = pair_rows(tmp, a + b, by1)

    def to_level1(dst):
        value = dot(t0[...].reshape(bx1 * by1, nz), r_fine)
        dst[HX1 : HX1 + bx1, ROWS : ROWS + by1] = value.reshape(bx1, by1, LANES)

    def to_level2(get, dst):
        for i in range(bx2):
            t1[i * by2 : (i + 1) * by2] = pair_rows(tmp, get(2 * i) + get(2 * i + 1), by2)
        n = bx2 * by2 // 2
        dst[px, py] = dot(t1[0:n], r_low) + dot(t1[n : 2 * n], r_high)

    own_copies[0].wait()
    loop(0, bx1, own_mobility)
    to_level1(m1)
    m1_start, m1_arrive, m1_sent = halo(m1, (HX1, ROWS), m1, HX1, (bx1, by1), s1, r1, 0)
    f1_start, f1_arrive, f1_sent = halo(f1, (HX1, ROWS), f1, HX1, (bx1, by1), s1, r1, 8)
    m1_start()
    to_level2(lambda i: m1[HX1 + i, ROWS : ROWS + by1], gm)
    ma_start, ma_arrive, ma_sent = along(1, gm, sa, ra, 0)
    fa_start, fa_arrive, fa_sent = along(1, gf, sa, ra, py_count - 1)
    mb_start, mb_arrive, mb_sent = along(0, gm, sb, rb, 0)
    fb_start, fb_arrive, fb_sent = along(0, gf, sb, rb, px_count - 1)
    ma_start()

    wide0, wide1, wide2, wide3 = (l[0].shape[0] for l in (l0, l1, l2, l3))
    y0, y1 = l0[0].shape[1], l1[0].shape[1]
    level0 = Level(l0, 1.0, px * bx - HX0, nx, (py * by - HY0, ny), (nz, nz), (1, wide0 - 1), False)
    level1 = Level(l1, 0.25, px * bx1 - HX1, nx // 2, (py * by1 - ROWS, ny // 2),
                   (nz // 2, LANES), (1, wide1 - 1), False)
    level2 = Level(l2, 0.25**2, -PAD2, nx // 4, (0, ny // 4), (nz // 4, half),
                   (PAD2, wide2 - PAD2), True)
    level3 = Level(l3, 0.25**3, -1, nx // 8, (0, ny // 8), (nz // 8, half), (1, wide3 - 1), True)
    for level in (level0, level1, level2, level3):
        level.clear(level.u)
        if level is not level1:
            level.clear(level.g)

    den_arrive()
    src_arrive()
    own_copies[1].wait()
    trim = slice(ROWS - HY0, ROWS - HY0 + y0)

    def invert(x):
        l0[0][x] = 1.0 / den[x, trim]

    loop(0, wide0, invert)
    level0.setup()

    def scale0(x):
        l0[5][x] = l0[4][x] * src[x, trim]

    loop(1, wide0 - 1, scale0)
    level0.sweep(level0.g, level0.u)

    def restrict0(i):
        x = HX0 + 2 * i
        both = level0.residual(x) + level0.residual(x + 1)
        t0[i] = pair_rows(tmp, both[HY0 : HY0 + by], by1)

    loop(0, bx1, restrict0)
    to_level1(f1)
    f1_start()

    ma_arrive()
    mb_start()
    m1_arrive()
    m1_sent()
    level1.setup()
    f1_arrive()
    f1_sent()

    def scale1(x):
        f1[x] = l1[4][x] * f1[x]

    loop(1, wide1 - 1, scale1)
    f1[0] = jnp.zeros(level1.shape, jnp.float32)
    f1[wide1 - 1] = jnp.zeros(level1.shape, jnp.float32)
    level1.sweep(level1.g, level1.u)
    to_level2(lambda i: level1.residual(HX1 + i)[ROWS : ROWS + by1], gf)
    fa_start()

    def spread(gathered, dst):
        n = bx2 // 2
        lane = iota((n * by2, LANES), 1)
        groups = py_count // 2

        def body(p):
            for q in range(groups):
                a, b = gathered[p, q], gathered[p, q + groups]
                first = jnp.where(lane < half, a, pltpu.roll(b, half, 1))
                second = jnp.where(lane < half, pltpu.roll(a, half, 1), b)
                for i in range(n):
                    rows = slice(q * by2, (q + 1) * by2)
                    piece = slice(i * by2, (i + 1) * by2)
                    dst[PAD2 + p * bx2 + i, rows] = first[piece]
                    dst[PAD2 + p * bx2 + n + i, rows] = second[piece]

        loop(0, px_count, body)

    def pair2(get, dst):
        count = wide3 - 2
        rows = l3[0].shape[1]

        def body(i):
            t2[i] = pair_rows(tmp, get(PAD2 + 2 * i) + get(PAD2 + 2 * i + 1), rows)

        loop(0, count, body)
        dst[1 : 1 + count] = dot(t2[...].reshape(count * rows, LANES), r_pack).reshape(
            count, rows, LANES
        )

    mb_arrive()
    one2 = jnp.ones((PAD2,) + level2.shape, jnp.float32)
    one3 = jnp.ones(level3.shape, jnp.float32)
    m2, m3 = l2[0], l3[0]
    spread(gm, m2)
    m2[0:PAD2] = one2
    m2[wide2 - PAD2 :] = one2
    level2.setup()
    pair2(lambda x: m2[x], m3)
    m3[0] = one3
    m3[wide3 - 1] = one3

    def mend3(x):
        m3[x] = jnp.where(level3.gz < level3.nz, m3[x], 1.0)

    loop(1, wide3 - 1, mend3)
    level3.setup()

    fa_arrive()
    fb_start()
    fb_arrive()
    f2, f3 = l2[5], l3[5]
    spread(gf, f2)

    def scale2(x):
        f2[x] = l2[4][x] * f2[x]

    loop(PAD2, wide2 - PAD2, scale2)
    level2.sweep(level2.g, level2.u)
    pair2(level2.residual, f3)

    def scale3(x):
        f3[x] = l3[4][x] * f3[x]

    loop(1, wide3 - 1, scale3)

    m3[0] = jnp.zeros(level3.shape, jnp.float32)
    m3[wide3 - 1] = jnp.zeros(level3.shape, jnp.float32)
    level3.sweep(f3, level3.u)
    now, later = level3.u, m3
    for _ in range(COARSE - 2):
        level3.sweep(now, later)
        now, later = later, now

    p_pack = matrix(
        (LANES, LANES), lambda k, z: (z // half == k // half) & ((z % half) // 2 == k % half), 1.0
    )
    count3, rows3 = wide3 - 2, l3[0].shape[1]
    pe2[...] = dot(now[1 : 1 + count3].reshape(count3 * rows3, LANES), p_pack).reshape(
        count3, rows3, LANES
    )

    def add2(i):
        wide = double_rows(tmp, pe2[i])
        for j in range(2):
            x = PAD2 + 2 * i + j
            level2.u[x] = level2.u[x] + wide

    loop(0, count3, add2)
    zero2 = jnp.zeros((PAD2,) + level2.shape, jnp.float32)
    m2[0:PAD2] = zero2
    m2[wide2 - PAD2 :] = zero2
    level2.u[0:PAD2] = zero2
    level2.u[wide2 - PAD2 :] = zero2
    level2.sweep(level2.u, m2)
    level2.sweep(m2, level2.u)

    full = 2 * level2.shape[0]
    shift = lax.rem(full + ROWS // 2 - py * by2, full)
    take = pe1.shape[1]

    def fetch(c):
        e = level2.u[px * bx2 + c]
        both = jnp.concatenate([e, pltpu.roll(e, half, 1)], 0)
        pe1[c] = pltpu.roll(both, shift, 0)[0:take]

    loop(0, wide1 // 2, fetch)
    p_one = matrix((LANES, LANES), lambda k, z: z // 2 == k, 1.0)
    pe1[...] = dot(pe1[...].reshape(-1, LANES), p_one).reshape(pe1.shape)

    def add1(i):
        wide = double_rows(tmp, pe1[i][0 : y1 // 2])
        for j in range(2):
            x = 2 * i + j
            level1.u[x] = level1.u[x] + wide

    loop(0, wide1 // 2, add1)
    m1[0] = jnp.zeros(level1.shape, jnp.float32)
    m1[wide1 - 1] = jnp.zeros(level1.shape, jnp.float32)
    level1.sweep(level1.u, m1)
    level1.sweep(m1, level1.u)

    p_zero = matrix((LANES, nz), lambda k, z: z // 2 == k, 1.0)
    base = HX1 - HX0 // 2
    count = wide0 // 2
    pe0[...] = dot(level1.u[base : base + count].reshape(count * y1, LANES), p_zero).reshape(pe0.shape)

    def add0(i):
        low = ROWS - HY0 // 2
        wide = double_rows(tmp, pe0[i, low : low + y0 // 2])
        for j in range(2):
            x = 2 * i + j
            level0.u[x] = level0.u[x] + wide

    loop(0, count, add0)
    m0 = l0[0]
    level0.sweep(level0.u, m0)

    def last(x):
        v, rest = level0.change(m0, HX0 + x)
        out[x] = (0.2 * v + rest)[HY0 : HY0 + by]

    loop(0, bx, last, 2)

    for done in (den_sent, src_sent, ma_sent, mb_sent, fa_sent, fb_sent):
        done()


def per_device(px_count, py_count, source, density):
    bx, by, nz = source.shape
    f32 = jnp.float32
    bx1, by1, bx2, by2 = bx // 2, by // 2, bx // 4, by // 4

    def level(wide, rows, lanes):
        return [pltpu.VMEM((wide, rows, lanes), f32)] * 7

    y0, y1 = by + 2 * HY0, by1 + 2 * ROWS
    wide0, wide1 = bx + 2 * HX0, bx1 + 2 * HX1
    x2, rows2 = bx2 * px_count, by2 * py_count // 2
    ext = pltpu.VMEM((wide0, by + 2 * ROWS, nz), f32)
    take = -(-(y1 // 2) // ROWS) * ROWS
    gather = pltpu.VMEM((px_count, py_count, bx2 * by2 // 2, LANES), f32)
    scratch = [
        ext,
        ext,
        level(wide0, y0, nz),
        level(wide1, y1, LANES),
        level(x2 + 2 * PAD2, rows2, LANES),
        level(x2 // 2 + 2, rows2 // 2, LANES),
        pltpu.VMEM((wide0 // 2, y1, nz), f32),
        pltpu.VMEM((wide1 // 2, take, LANES), f32),
        pltpu.VMEM((x2 // 2, rows2 // 2, LANES), f32),
        pltpu.VMEM((bx1, by1, nz), f32),
        pltpu.VMEM((bx2 * by2, LANES), f32),
        pltpu.VMEM((x2 // 2, rows2 // 2, LANES), f32),
        pltpu.VMEM((nz // LANES, max(y0, y1, rows2), LANES), f32),
        gather,
        gather,
        pltpu.SemaphoreType.DMA((2,)),
        pltpu.SemaphoreType.DMA((16,)),
        pltpu.SemaphoreType.DMA((16,)),
        pltpu.SemaphoreType.DMA((16,)),
        pltpu.SemaphoreType.DMA((16,)),
        pltpu.SemaphoreType.DMA((2 * (py_count - 1),)),
        pltpu.SemaphoreType.DMA((2 * (py_count - 1),)),
        pltpu.SemaphoreType.DMA((2 * (px_count - 1),)),
        pltpu.SemaphoreType.DMA((2 * (px_count - 1),)),
    ]
    return pl.pallas_call(
        functools.partial(kernel, (px_count, py_count)),
        out_shape=jax.ShapeDtypeStruct(source.shape, f32),
        in_specs=[pl.BlockSpec(memory_space=pl.ANY)] * 2,
        out_specs=pl.BlockSpec(memory_space=pltpu.VMEM),
        scratch_shapes=scratch,
        compiler_params=pltpu.CompilerParams(
            collective_id=0, has_side_effects=True, vmem_limit_bytes=56 * 1024 * 1024
        ),
    )(source, density)


def solution(mesh):
    spec = P("px", "py", None)
    return jax.shard_map(
        functools.partial(per_device, mesh.shape["px"], mesh.shape["py"]),
        mesh=mesh,
        in_specs=(spec, spec),
        out_specs=spec,
        check_vma=False,
    )
```

```python
import functools

import jax
import jax.numpy as jnp
from jax import lax
from jax.experimental import pallas as pl
from jax.experimental.pallas import tpu as pltpu
from jax.sharding import PartitionSpec as P

COARSE = 8
LANES = 128
HX0, HY0, HX1, PAD2 = 4, 4, 6, 3
ROWS = 8
DIRECTIONS = [(dx, dy) for dx in (-1, 0, 1) for dy in (-1, 0, 1) if (dx, dy) != (0, 0)]
MESH = pl.DeviceIdType.MESH


def iota(shape, dim):
    return lax.broadcasted_iota(jnp.int32, shape, dim)


def dot(a, b):
    return jnp.dot(a, b, precision=lax.Precision.HIGHEST, preferred_element_type=jnp.float32)


def matrix(shape, test, value):
    return jnp.where(test(iota(shape, 0), iota(shape, 1)), value, 0.0).astype(jnp.float32)


def loop(low, high, body, unroll=1):
    def step(i, carry):
        body(i)
        return carry

    lax.fori_loop(low, high, step, 0, unroll=unroll)


def chunks(low, high, size, most, body):
    count = high - low
    n = max(d for d in range(1, count + 1) if count % d == 0 and (d == 1 or d * size <= most))
    if n == count:
        body(low, n)
    else:
        loop(0, count // n, lambda i: body(low + i * n, n))


class Level:
    def __init__(self, refs, factor, start, total, rows, lanes, span, packed):
        (self.m, self.wx, self.wy, self.wz, self.k, self.g, self.u) = refs
        self.low, self.high = span
        self.half = 0.5 * factor
        self.start, self.total = start, total
        shape = self.m.shape[1:]
        self.shape, self.packed = shape, packed
        row, lane = iota(shape, 0), iota(shape, 1)
        first, total_y = rows
        nz, stride = lanes
        group = lane // stride if packed else 0
        gy = first + row + group * shape[0]
        gz = lane % stride if packed else lane
        self.row = row
        self.size = -(-shape[0] // ROWS) * (shape[1] // LANES)

        def keep(pos, count, span):
            plus = (pos != count - 1) & (pos != -1) & (pos != span - 1)
            minus = (pos != 0) & (pos != count)
            return jnp.where(plus, 1.0, 0.0), jnp.where(minus, 1.0, 0.0)

        self.kyp, self.kym = keep(gy, total_y, -9)
        self.kzp, self.kzm = keep(gz, nz, stride)
        self.gz, self.nz = gz, nz

    def y_minus(self, t):
        r = pltpu.roll(t, 1, t.ndim - 2)
        if self.packed:
            r = jnp.where(self.row == 0, pltpu.roll(r, LANES // 2, r.ndim - 1), r)
        return r

    def y_plus(self, t):
        r = pltpu.roll(t, self.shape[0] - 1, t.ndim - 2)
        if self.packed:
            r = jnp.where(self.row == self.shape[0] - 1, pltpu.roll(r, LANES // 2, r.ndim - 1), r)
        return r

    def z_minus(self, t):
        return pltpu.roll(t, 1, t.ndim - 1)

    def z_plus(self, t):
        return pltpu.roll(t, self.shape[1] - 1, t.ndim - 1)

    def clear(self, *refs):
        for i in (self.low - 1, self.high):
            for ref in refs:
                ref[i] = jnp.zeros(self.shape, jnp.float32)

    def face(self, x):
        gx = self.start + x
        return jnp.where((gx != self.total - 1) & (gx != -1), 1.0, 0.0)

    def setup(self, source=None):
        before = self.low - 1
        self.wx[before] = (self.half * self.face(before)) * (self.m[before] + self.m[self.low])
        known = self.kyp + self.kym + self.kzp + self.kzm

        def body(x, n):
            m = [self.m[x - 1 + j] for j in range(n + 2)]
            f = None if source is None else [source(x + j) for j in range(n)]
            k = [self.face(x - 1 + j) for j in range(n + 1)]
            s = [k[j] * (m[j] + m[j + 1]) for j in range(n + 1)]
            done = []
            for j in range(n):
                c = m[j + 1]
                wyp = self.kyp * (c + self.y_plus(c))
                wym = self.kym * (c + self.y_minus(c))
                wzp = self.kzp * (c + self.z_plus(c))
                wzm = self.kzm * (c + self.z_minus(c))
                missing = 6.0 - (k[j] + k[j + 1]) - known
                diag = ((s[j] + s[j + 1]) + (wyp + wym)) + ((wzp + wzm) + 2.0 * c * missing)
                done.append((self.half * s[j + 1], self.half * wyp, self.half * wzp,
                             0.8 / (self.half * diag)))
            for j, (wx, wy, wz, inverse) in enumerate(done):
                self.wx[x + j] = wx
                self.wy[x + j] = wy
                self.wz[x + j] = wz
                self.k[x + j] = inverse
                if f is not None:
                    self.g[x + j] = inverse * f[j]

        chunks(self.low, self.high, self.size, 12, body)

    def scale(self):
        def body(x, n):
            at = pl.ds(x, n)
            self.g[at] = self.k[at] * self.g[at]

        chunks(self.low, self.high, self.size, 24, body)

    def change(self, ref, x, n):
        at = pl.ds(x, n)
        v, wy, wz = ref[at], self.wy[at], self.wz[at]
        total = self.wx[at] * ref[pl.ds(x + 1, n)] + self.wx[pl.ds(x - 1, n)] * ref[pl.ds(x - 1, n)]
        total = total + (wy * self.y_plus(v) + self.y_minus(wy * v))
        total = total + (wz * self.z_plus(v) + self.z_minus(wz * v))
        return v, self.g[at] + self.k[at] * total

    def sweep(self, src, dst, inset=0):
        def body(x, n):
            v, rest = self.change(src, x, n)
            dst[pl.ds(x, n)] = 0.2 * v + rest

        chunks(self.low + inset, self.high - inset, self.size, 24, body)

    def residual(self, x, n):
        v, rest = self.change(self.u, x, n)
        return (rest - 0.8 * v) / self.k[pl.ds(x, n)]


def columns(width):
    return [slice(c, c + LANES) for c in range(0, width, LANES)]


def pair_slabs(tmp, i, value):
    count, rows, width = value.shape
    sums = [value[j] + value[j + 1] for j in range(0, count, 2)]
    for j, both in enumerate(sums):
        for k, c in enumerate(columns(width)):
            tmp[k, i + j, 0:rows] = both[:, c]


def pair_rows(tmp, count, rows, width):
    parts = [
        tmp[k, 0:count, pl.ds(0, rows, stride=2)] + tmp[k, 0:count, pl.ds(1, rows, stride=2)]
        for k in range(width // LANES)
    ]
    return parts[0] if len(parts) == 1 else jnp.concatenate(parts, 2)


def add_double(tmp, value, target, first, size):
    count, rows, width = value.shape
    for k, c in enumerate(columns(width)):
        tmp[k, 0:count, pl.ds(0, rows, stride=2)] = value[:, :, c]
        tmp[k, 0:count, pl.ds(1, rows, stride=2)] = value[:, :, c]

    def body(i, n):
        parts = [tmp[k, pl.ds(i, n), 0 : 2 * rows] for k in range(width // LANES)]
        e = parts[0] if len(parts) == 1 else jnp.concatenate(parts, 2)
        old = target[pl.ds(first + 2 * i, 2 * n)]
        new = [old[j] + e[j // 2] for j in range(2 * n)]
        for j in range(2 * n):
            target[first + 2 * i + j] = new[j]

    chunks(0, count, 2 * size, 24, body)


def kernel(sizes, source, density, out, den, src, l0, l1, l2, l3, pe0, pe1, t1, tmp,
           gm, gf, copy_sem, s0, r0, s1, r1, sa, ra, sb, rb):
    px_count, py_count = sizes
    px, py = lax.axis_index("px"), lax.axis_index("py")
    bx, by, nz = source.shape
    nx, ny = bx * px_count, by * py_count
    bx1, by1, bx2, by2 = bx // 2, by // 2, bx // 4, by // 4

    def inside(dx, dy):
        test = None
        for d, pos, count in ((dx, px, px_count), (dy, py, py_count)):
            if d:
                one = (pos < count - 1) if d > 0 else (pos > 0)
                test = one if test is None else test & one
        return test

    def fill(ref, hx, value):
        wide, rows = ref.shape[0], ref.shape[1]

        @pl.when(px == 0)
        def _():
            ref[0:hx] = jnp.full((hx,) + ref.shape[1:], value, jnp.float32)

        @pl.when(px == px_count - 1)
        def _():
            ref[wide - hx :] = jnp.full((hx,) + ref.shape[1:], value, jnp.float32)

        @pl.when(py == 0)
        def _():
            ref[:, 0:ROWS] = jnp.full((wide, ROWS, ref.shape[2]), value, jnp.float32)

        @pl.when(py == py_count - 1)
        def _():
            ref[:, rows - ROWS :] = jnp.full((wide, ROWS, ref.shape[2]), value, jnp.float32)

    def halo(src_ref, offset, dst_ref, hx, block, send, recv, base):
        def part(d, own, count, width, at):
            if d == 0:
                return pl.ds(at, count), pl.ds(width, count)
            if d > 0:
                return pl.ds(at + count - width, width), pl.ds(0, width)
            return pl.ds(at, width), pl.ds(width + count, width)

        def copies(n, dx, dy):
            sx, tx = part(dx, None, block[0], hx, offset[0])
            sy, ty = part(dy, None, block[1], ROWS, offset[1])
            return pltpu.make_async_remote_copy(
                src_ref=src_ref.at[sx, sy],
                dst_ref=dst_ref.at[tx, ty],
                send_sem=send.at[base + n],
                recv_sem=recv.at[base + n],
                device_id=(px + dx, py + dy),
                device_id_type=MESH,
            )

        def start():
            for n, (dx, dy) in enumerate(DIRECTIONS):
                @pl.when(inside(dx, dy))
                def _():
                    copies(n, dx, dy).start()

        def arrive():
            for n, (dx, dy) in enumerate(DIRECTIONS):
                @pl.when(inside(-dx, -dy))
                def _():
                    copies(n, dx, dy).wait_recv()

        def sent():
            for n, (dx, dy) in enumerate(DIRECTIONS):
                @pl.when(inside(dx, dy))
                def _():
                    copies(n, dx, dy).wait_send()

        return start, arrive, sent

    def along(axis, ref, send, recv, base):
        count, me = (py_count, py) if axis else (px_count, px)
        region = ref.at[px, py] if axis else ref.at[px]

        def each(act):
            for k in range(1, count):
                to = lax.rem(me + k, count)
                act(pltpu.make_async_remote_copy(
                    src_ref=region,
                    dst_ref=region,
                    send_sem=send.at[base + k - 1],
                    recv_sem=recv.at[base + k - 1],
                    device_id=(px, to) if axis else (to, py),
                    device_id_type=MESH,
                ))

        def arrive():
            for k in range(1, count):
                frm = lax.rem(me + count - k, count)
                landed = ref.at[px, frm] if axis else ref.at[frm]
                pltpu.make_async_remote_copy(
                    src_ref=landed,
                    dst_ref=landed,
                    send_sem=send.at[base + k - 1],
                    recv_sem=recv.at[base + k - 1],
                    device_id=(px, frm) if axis else (frm, py),
                    device_id_type=MESH,
                ).wait_recv()

        return (lambda: each(lambda c: c.start())), arrive, (lambda: each(lambda c: c.wait_send()))

    m1, f1 = l1[0], l1[5]
    own_copies = [
        pltpu.make_async_copy(a, b.at[pl.ds(HX0, bx), pl.ds(ROWS, by)], copy_sem.at[i])
        for i, (a, b) in enumerate(((density, den), (source, src)))
    ]
    for c in own_copies:
        c.start()
    fill(m1, HX1, 1.0)
    fill(f1, HX1, 0.0)
    fill(den, HX0, 1.0)
    fill(src, HX0, 0.0)

    barrier = pltpu.get_barrier_semaphore()
    for k in range(1, py_count):
        pl.semaphore_signal(barrier, 1, device_id=(px, lax.rem(py + k, py_count)), device_id_type=MESH)
    for k in range(1, px_count):
        pl.semaphore_signal(barrier, 1, device_id=(lax.rem(px + k, px_count), py), device_id_type=MESH)
    for dx, dy in DIRECTIONS:
        if dx and dy:
            @pl.when(inside(dx, dy))
            def _():
                pl.semaphore_signal(barrier, 1, device_id=(px + dx, py + dy), device_id_type=MESH)
    beside_x = jnp.minimum(px, 1) + jnp.minimum(px_count - 1 - px, 1)
    beside_y = jnp.minimum(py, 1) + jnp.minimum(py_count - 1 - py, 1)
    pl.semaphore_wait(barrier, px_count + py_count - 2 + beside_x * beside_y)

    den_start, den_arrive, den_sent = halo(density, (0, 0), den, HX0, (bx, by), s0, r0, 0)
    src_start, src_arrive, src_sent = halo(source, (0, 0), src, HX0, (bx, by), s0, r0, 8)
    den_start()
    src_start()

    r_fine = matrix((nz, LANES), lambda z, c: z // 2 == c, 0.125)
    r_low = matrix((LANES, LANES), lambda z, c: z // 2 == c, 0.125)
    r_high = matrix((LANES, LANES), lambda z, c: z // 2 + LANES // 2 == c, 0.125)
    half = LANES // 2
    r_pack = matrix(
        (LANES, LANES), lambda z, c: (z // half == c // half) & ((z % half) // 2 == c % half), 0.125
    )

    def restrict0(get, dst):
        def body(i, n):
            pair_slabs(tmp, i, get(HX0 + 2 * i, 2 * n))

        chunks(0, bx1, 2 * (y0 // ROWS) * (nz // LANES), 24, body)
        value = dot(pair_rows(tmp, bx1, by1, nz).reshape(bx1 * by1, nz), r_fine)
        dst[HX1 : HX1 + bx1, ROWS : ROWS + by1] = value.reshape(bx1, by1, LANES)

    def restrict1(get, dst):
        def body(i, n):
            pair_slabs(tmp, i, get(HX1 + 2 * i, 2 * n))

        chunks(0, bx2, 2 * (y1 // ROWS), 24, body)
        sums = pair_rows(tmp, bx2, by2, LANES)
        for i in range(bx2):
            t1[i * by2 : (i + 1) * by2] = sums[i]
        n = bx2 * by2 // 2
        dst[px, py] = dot(t1[0:n], r_low) + dot(t1[n : 2 * n], r_high)

    wide0, wide1, wide2, wide3 = (l[0].shape[0] for l in (l0, l1, l2, l3))
    y0, y1 = l0[0].shape[1], l1[0].shape[1]
    own_copies[0].wait()
    restrict0(lambda x, n: 1.0 / den[pl.ds(x, n), ROWS : ROWS + by], m1)
    m1_start, m1_arrive, m1_sent = halo(m1, (HX1, ROWS), m1, HX1, (bx1, by1), s1, r1, 0)
    f1_start, f1_arrive, f1_sent = halo(f1, (HX1, ROWS), f1, HX1, (bx1, by1), s1, r1, 8)
    m1_start()
    restrict1(lambda x, n: m1[pl.ds(x, n), ROWS : ROWS + by1], gm)
    ma_start, ma_arrive, ma_sent = along(1, gm, sa, ra, 0)
    fa_start, fa_arrive, fa_sent = along(1, gf, sa, ra, py_count - 1)
    mb_start, mb_arrive, mb_sent = along(0, gm, sb, rb, 0)
    fb_start, fb_arrive, fb_sent = along(0, gf, sb, rb, px_count - 1)
    ma_start()

    level0 = Level(l0, 1.0, px * bx - HX0, nx, (py * by - HY0, ny), (nz, nz), (1, wide0 - 1), False)
    level1 = Level(l1, 0.25, px * bx1 - HX1, nx // 2, (py * by1 - ROWS, ny // 2),
                   (nz // 2, LANES), (2, wide1 - 2), False)
    level2 = Level(l2, 0.25**2, -PAD2, nx // 4, (0, ny // 4), (nz // 4, half),
                   (PAD2, wide2 - PAD2), True)
    level3 = Level(l3, 0.25**3, -1, nx // 8, (0, ny // 8), (nz // 8, half), (1, wide3 - 1), True)
    for level in (level0, level1, level2, level3):
        level.clear(level.u)
        if level is not level1:
            level.clear(level.g)

    den_arrive()
    src_arrive()
    own_copies[1].wait()
    trim = slice(ROWS - HY0, ROWS - HY0 + y0)

    def invert(x, n):
        at = pl.ds(x, n)
        l0[0][at] = 1.0 / den[at, trim]

    chunks(0, wide0, level0.size, 24, invert)
    level0.setup(lambda x: src[x, trim])
    level0.sweep(level0.g, level0.u, 1)
    restrict0(lambda x, n: level0.residual(x, n)[:, HY0 : HY0 + by], f1)
    f1_start()

    ma_arrive()
    mb_start()
    m1_arrive()
    m1_sent()
    level1.setup()
    f1_arrive()
    f1_sent()

    level1.scale()
    level1.clear(f1)
    level1.sweep(level1.g, level1.u)
    restrict1(lambda x, n: level1.residual(x, n)[:, ROWS : ROWS + by1], gf)
    fa_start()

    def spread(gathered, dst):
        n = bx2 // 2
        lane = iota((n * by2, LANES), 1)
        groups = py_count // 2

        def body(p):
            for q in range(groups):
                a, b = gathered[p, q], gathered[p, q + groups]
                first = jnp.where(lane < half, a, pltpu.roll(b, half, 1))
                second = jnp.where(lane < half, pltpu.roll(a, half, 1), b)
                for i in range(n):
                    rows = slice(q * by2, (q + 1) * by2)
                    piece = slice(i * by2, (i + 1) * by2)
                    dst[PAD2 + p * bx2 + i, rows] = first[piece]
                    dst[PAD2 + p * bx2 + n + i, rows] = second[piece]

        loop(0, px_count, body)

    def pair2(get, dst):
        count = wide3 - 2
        rows = l3[0].shape[1]

        def body(i, n):
            pair_slabs(tmp, i, get(PAD2 + 2 * i, 2 * n))

        chunks(0, count, 2 * level2.size, 24, body)
        sums = pair_rows(tmp, count, rows, LANES)
        dst[1 : 1 + count] = dot(sums.reshape(count * rows, LANES), r_pack).reshape(
            count, rows, LANES
        )

    mb_arrive()
    one2 = jnp.ones((PAD2,) + level2.shape, jnp.float32)
    one3 = jnp.ones(level3.shape, jnp.float32)
    m2, m3 = l2[0], l3[0]
    spread(gm, m2)
    m2[0:PAD2] = one2
    m2[wide2 - PAD2 :] = one2
    level2.setup()
    pair2(lambda x, n: m2[pl.ds(x, n)], m3)
    m3[0] = one3
    m3[wide3 - 1] = one3

    inner3 = slice(1, wide3 - 1)
    m3[inner3] = jnp.where(level3.gz < level3.nz, m3[inner3], 1.0)
    level3.setup()

    fa_arrive()
    fb_start()
    fb_arrive()
    f2, f3 = l2[5], l3[5]
    spread(gf, f2)

    level2.scale()
    level2.sweep(level2.g, level2.u)
    pair2(level2.residual, f3)

    level3.scale()
    m3[0] = jnp.zeros(level3.shape, jnp.float32)
    m3[wide3 - 1] = jnp.zeros(level3.shape, jnp.float32)
    level3.sweep(f3, level3.u)
    now, later = level3.u, m3
    for _ in range(COARSE - 2):
        level3.sweep(now, later)
        now, later = later, now

    p_pack = matrix(
        (LANES, LANES), lambda k, z: (z // half == k // half) & ((z % half) // 2 == k % half), 1.0
    )
    count3, rows3 = wide3 - 2, l3[0].shape[1]
    e3 = dot(now[1 : 1 + count3].reshape(count3 * rows3, LANES), p_pack)
    add_double(tmp, e3.reshape(count3, rows3, LANES), level2.u, PAD2, level2.size)
    zero2 = jnp.zeros((PAD2,) + level2.shape, jnp.float32)
    m2[0:PAD2] = zero2
    m2[wide2 - PAD2 :] = zero2
    level2.u[0:PAD2] = zero2
    level2.u[wide2 - PAD2 :] = zero2
    level2.sweep(level2.u, m2)
    level2.sweep(m2, level2.u)

    full = 2 * level2.shape[0]
    shift = lax.rem(full + ROWS // 2 - py * by2, full)
    take = pe1.shape[1]

    def fetch(c, n):
        e = [level2.u[px * bx2 + c + j] for j in range(n)]
        e = [jnp.concatenate([one, pltpu.roll(one, half, 1)], 0) for one in e]
        e = [pltpu.roll(one, shift, 0)[0:take] for one in e]
        for j in range(n):
            pe1[c + j] = e[j]

    chunks(0, wide1 // 2, 2 * level2.size, 32, fetch)
    p_one = matrix((LANES, LANES), lambda k, z: z // 2 == k, 1.0)
    e2 = dot(pe1[...].reshape(-1, LANES), p_one).reshape(pe1.shape)
    add_double(tmp, e2[:, 0 : y1 // 2], level1.u, 0, level1.size)
    level1.sweep(level1.u, m1)
    level1.sweep(m1, level1.u)

    p_zero = matrix((LANES, nz), lambda k, z: z // 2 == k, 1.0)
    base = HX1 - HX0 // 2
    count = wide0 // 2
    e1 = dot(level1.u[base : base + count].reshape(count * y1, LANES), p_zero)
    pe0[...] = e1.reshape(pe0.shape)
    low = ROWS - HY0 // 2
    add_double(tmp, pe0[:, low : low + y0 // 2], level0.u, 0, level0.size)
    m0 = l0[0]
    level0.sweep(level0.u, m0, 2)

    def last(x, n):
        v, rest = level0.change(m0, HX0 + x, n)
        out[pl.ds(x, n)] = (0.2 * v + rest)[:, HY0 : HY0 + by]

    chunks(0, bx, level0.size, 24, last)

    for done in (den_sent, src_sent, ma_sent, mb_sent, fa_sent, fb_sent):
        done()


def per_device(px_count, py_count, source, density):
    bx, by, nz = source.shape
    f32 = jnp.float32
    bx1, by1, bx2, by2 = bx // 2, by // 2, bx // 4, by // 4

    def level(wide, rows, lanes):
        return [pltpu.VMEM((wide, rows, lanes), f32)] * 7

    y0, y1 = by + 2 * HY0, by1 + 2 * ROWS
    wide0, wide1 = bx + 2 * HX0, bx1 + 2 * HX1
    x2, rows2 = bx2 * px_count, by2 * py_count // 2
    ext = pltpu.VMEM((wide0, by + 2 * ROWS, nz), f32)
    take = -(-(y1 // 2) // ROWS) * ROWS
    gather = pltpu.VMEM((px_count, py_count, bx2 * by2 // 2, LANES), f32)
    scratch = [
        ext,
        ext,
        level(wide0, y0, nz),
        level(wide1, y1, LANES),
        level(x2 + 2 * PAD2, rows2, LANES),
        level(x2 // 2 + 2, rows2 // 2, LANES),
        pltpu.VMEM((wide0 // 2, y1, nz), f32),
        pltpu.VMEM((wide1 // 2, take, LANES), f32),
        pltpu.VMEM((bx2 * by2, LANES), f32),
        pltpu.VMEM((nz // LANES, max(wide0, wide1, x2) // 2, max(y0, y1, rows2), LANES), f32),
        gather,
        gather,
        pltpu.SemaphoreType.DMA((2,)),
        pltpu.SemaphoreType.DMA((16,)),
        pltpu.SemaphoreType.DMA((16,)),
        pltpu.SemaphoreType.DMA((16,)),
        pltpu.SemaphoreType.DMA((16,)),
        pltpu.SemaphoreType.DMA((2 * (py_count - 1),)),
        pltpu.SemaphoreType.DMA((2 * (py_count - 1),)),
        pltpu.SemaphoreType.DMA((2 * (px_count - 1),)),
        pltpu.SemaphoreType.DMA((2 * (px_count - 1),)),
    ]
    return pl.pallas_call(
        functools.partial(kernel, (px_count, py_count)),
        out_shape=jax.ShapeDtypeStruct(source.shape, f32),
        in_specs=[pl.BlockSpec(memory_space=pl.ANY)] * 2,
        out_specs=pl.BlockSpec(memory_space=pltpu.VMEM),
        scratch_shapes=scratch,
        compiler_params=pltpu.CompilerParams(
            collective_id=0, has_side_effects=True, vmem_limit_bytes=56 * 1024 * 1024
        ),
    )(source, density)


def solution(mesh):
    spec = P("px", "py", None)
    return jax.shard_map(
        functools.partial(per_device, mesh.shape["px"], mesh.shape["py"]),
        mesh=mesh,
        in_specs=(spec, spec),
        out_specs=spec,
        check_vma=False,
    )
```

```python
import functools

import jax
import jax.numpy as jnp
from jax import lax
from jax.experimental import pallas as pl
from jax.experimental.pallas import tpu as pltpu
from jax.sharding import PartitionSpec as P

COARSE = 8
LANES = 128
HX0, HY0, HX1, PAD2 = 4, 4, 4, 2
THREE, TWO = ((0, 2), (2, 1)), ((0, 2),)
ROWS = 8
DIRECTIONS = [(dx, dy) for dx in (-1, 0, 1) for dy in (-1, 0, 1) if (dx, dy) != (0, 0)]
MESH = pl.DeviceIdType.MESH


def iota(shape, dim):
    return lax.broadcasted_iota(jnp.int32, shape, dim)


def dot(a, b):
    return jnp.dot(a, b, precision=lax.Precision.HIGHEST, preferred_element_type=jnp.float32)


def matrix(shape, test, value):
    return jnp.where(test(iota(shape, 0), iota(shape, 1)), value, 0.0).astype(jnp.float32)


def loop(low, high, body, unroll=1):
    def step(i, carry):
        body(i)
        return carry

    lax.fori_loop(low, high, step, 0, unroll=unroll)


def chunks(low, high, size, most, body):
    count = high - low
    n = max(d for d in range(1, count + 1) if count % d == 0 and (d == 1 or d * size <= most))
    if n == count:
        body(low, n)
    else:
        loop(0, count // n, lambda i: body(low + i * n, n))


class Level:
    def __init__(self, refs, factor, start, total, rows, lanes, span, packed):
        (self.m, self.wx, self.wy, self.wz, self.k, self.g, self.u) = refs
        self.low, self.high = span
        self.half = 0.5 * factor
        self.start, self.total = start, total
        shape = self.m.shape[1:]
        self.shape, self.packed = shape, packed
        row, lane = iota(shape, 0), iota(shape, 1)
        first, total_y = rows
        nz, stride = lanes
        group = lane // stride if packed else 0
        gy = first + row + group * shape[0]
        gz = lane % stride if packed else lane
        self.row = row
        self.size = -(-shape[0] // ROWS) * (shape[1] // LANES)

        def keep(pos, count, span):
            plus = (pos != count - 1) & (pos != -1) & (pos != span - 1)
            minus = (pos != 0) & (pos != count)
            return jnp.where(plus, 1.0, 0.0), jnp.where(minus, 1.0, 0.0)

        self.kyp, self.kym = keep(gy, total_y, -9)
        self.kzp, self.kzm = keep(gz, nz, stride)
        self.gz, self.nz = gz, nz

    def y_minus(self, t):
        r = pltpu.roll(t, 1, t.ndim - 2)
        if self.packed:
            r = jnp.where(self.row == 0, pltpu.roll(r, LANES // 2, r.ndim - 1), r)
        return r

    def y_plus(self, t):
        r = pltpu.roll(t, self.shape[0] - 1, t.ndim - 2)
        if self.packed:
            r = jnp.where(self.row == self.shape[0] - 1, pltpu.roll(r, LANES // 2, r.ndim - 1), r)
        return r

    def z_minus(self, t):
        return pltpu.roll(t, 1, t.ndim - 1)

    def z_plus(self, t):
        return pltpu.roll(t, self.shape[1] - 1, t.ndim - 1)

    def clear(self, *refs):
        for i in (self.low - 1, self.high):
            for ref in refs:
                ref[i] = jnp.zeros(self.shape, jnp.float32)

    def face(self, x):
        gx = self.start + x
        return jnp.where((gx != self.total - 1) & (gx != -1), 1.0, 0.0)

    def setup(self, source=None):
        before = self.low - 1
        self.wx[before] = (self.half * self.face(before)) * (self.m[before] + self.m[self.low])
        known = self.kyp + self.kym + self.kzp + self.kzm

        def body(x, n):
            m = [self.m[x - 1 + j] for j in range(n + 2)]
            f = None if source is None else [source(x + j) for j in range(n)]
            k = [self.face(x - 1 + j) for j in range(n + 1)]
            s = [k[j] * (m[j] + m[j + 1]) for j in range(n + 1)]
            done = []
            for j in range(n):
                c = m[j + 1]
                wyp = self.kyp * (c + self.y_plus(c))
                wym = self.kym * (c + self.y_minus(c))
                wzp = self.kzp * (c + self.z_plus(c))
                wzm = self.kzm * (c + self.z_minus(c))
                missing = 6.0 - (k[j] + k[j + 1]) - known
                diag = ((s[j] + s[j + 1]) + (wyp + wym)) + ((wzp + wzm) + 2.0 * c * missing)
                done.append((self.half * s[j + 1], self.half * wyp, self.half * wzp,
                             0.8 / (self.half * diag)))
            for j, (wx, wy, wz, inverse) in enumerate(done):
                self.wx[x + j] = wx
                self.wy[x + j] = wy
                self.wz[x + j] = wz
                self.k[x + j] = inverse
                if f is not None:
                    self.g[x + j] = inverse * f[j]

        chunks(self.low, self.high, self.size, 12, body)

    def scale(self):
        def body(x, n):
            at = pl.ds(x, n)
            self.g[at] = self.k[at] * self.g[at]

        chunks(self.low, self.high, self.size, 24, body)

    def change(self, ref, x, n):
        at = pl.ds(x, n)
        v, wy, wz = ref[at], self.wy[at], self.wz[at]
        total = self.wx[at] * ref[pl.ds(x + 1, n)] + self.wx[pl.ds(x - 1, n)] * ref[pl.ds(x - 1, n)]
        total = total + (wy * self.y_plus(v) + self.y_minus(wy * v))
        total = total + (wz * self.z_plus(v) + self.z_minus(wz * v))
        return v, self.g[at] + self.k[at] * total

    def sweep(self, src, dst, inset=0):
        def body(x, n):
            v, rest = self.change(src, x, n)
            dst[pl.ds(x, n)] = 0.2 * v + rest

        chunks(self.low + inset, self.high - inset, self.size, 24, body)

    def residual(self, x, n):
        v, rest = self.change(self.u, x, n)
        return (rest - 0.8 * v) / self.k[pl.ds(x, n)]


def columns(width):
    return [slice(c, c + LANES) for c in range(0, width, LANES)]


def pair_slabs(tmp, i, value):
    count, rows, width = value.shape
    sums = [value[j] + value[j + 1] for j in range(0, count, 2)]
    for j, both in enumerate(sums):
        for k, c in enumerate(columns(width)):
            tmp[k, i + j, 0:rows] = both[:, c]


def pair_rows(tmp, count, rows, width):
    parts = [
        tmp[k, 0:count, pl.ds(0, rows, stride=2)] + tmp[k, 0:count, pl.ds(1, rows, stride=2)]
        for k in range(width // LANES)
    ]
    return parts[0] if len(parts) == 1 else jnp.concatenate(parts, 2)


def add_double(tmp, value, target, first, size):
    count, rows, width = value.shape
    for k, c in enumerate(columns(width)):
        tmp[k, 0:count, pl.ds(0, rows, stride=2)] = value[:, :, c]
        tmp[k, 0:count, pl.ds(1, rows, stride=2)] = value[:, :, c]

    def body(i, n):
        parts = [tmp[k, pl.ds(i, n), 0 : 2 * rows] for k in range(width // LANES)]
        e = parts[0] if len(parts) == 1 else jnp.concatenate(parts, 2)
        old = target[pl.ds(first + 2 * i, 2 * n)]
        new = [old[j] + e[j // 2] for j in range(2 * n)]
        for j in range(2 * n):
            target[first + 2 * i + j] = new[j]

    chunks(0, count, 2 * size, 24, body)


def kernel(sizes, source, density, out, den, src, l0, l1, l2, l3, pe0, pe1, t1, tmp,
           gm, gf, copy_sem, halos, sa, ra, sb, rb):
    px_count, py_count = sizes
    px, py = lax.axis_index("px"), lax.axis_index("py")
    bx, by, nz = source.shape
    nx, ny = bx * px_count, by * py_count
    bx1, by1, bx2, by2 = bx // 2, by // 2, bx // 4, by // 4

    def inside(dx, dy):
        test = None
        for d, pos, count in ((dx, px, px_count), (dy, py, py_count)):
            if d:
                one = (pos < count - 1) if d > 0 else (pos > 0)
                test = one if test is None else test & one
        return test

    class Halo:
        def __init__(self, refs, hx, pieces, block):
            self.xsend, self.xland, self.ysend, self.yland, self.send, self.recv = refs
            self.hx, self.pieces, self.block = hx, pieces, block

        def fill(self, value):
            edges = ((px == 0, 0, 0), (px == px_count - 1, 0, 1),
                     (py == 0, 1, 0), (py == py_count - 1, 1, 1))
            hx, bx = self.hx, self.block[0]
            for test, dim, side in edges:
                @pl.when(test)
                def _():
                    if dim == 0:
                        ref = self.xland
                        ref[side] = jnp.full(ref.shape[1:], value, jnp.float32)
                    for ref in self.yland:
                        if dim:
                            ref[side] = jnp.full(ref.shape[1:], value, jnp.float32)
                        else:
                            at = side * (hx + bx)
                            for s in range(2):
                                ref[s, at : at + hx] = jnp.full((hx,) + ref.shape[2:], value, jnp.float32)

        def pack(self, ref, ox, oy):
            hx, (bx, by) = self.hx, self.block
            self.xsend[0] = ref[ox : ox + hx, oy : oy + by]
            self.xsend[1] = ref[ox + bx - hx : ox + bx, oy : oy + by]
            for ysend, (d, w) in zip(self.ysend, self.pieces):
                ysend[0] = ref[ox : ox + bx, oy + d : oy + d + w]
                ysend[1] = ref[ox : ox + bx, oy + by - d - w : oy + by - d]

        def each(self, act, sign):
            hx, bx = self.hx, self.block[0]
            n = 0
            for dx, dy in DIRECTIONS:
                if dy == 0:
                    side = (dx + 1) // 2
                    pairs = [(self.xsend.at[side], self.xland.at[1 - side])]
                else:
                    side = (dy + 1) // 2
                    own, there, count = ((0, hx + bx, hx), (0, hx, bx), (bx - hx, 0, hx))[dx + 1]
                    pairs = [
                        (a.at[side, pl.ds(own, count)], b.at[1 - side, pl.ds(there, count)])
                        for a, b in zip(self.ysend, self.yland)
                    ]
                copies = []
                for a, b in pairs:
                    copies.append(pltpu.make_async_remote_copy(
                        src_ref=a,
                        dst_ref=b,
                        send_sem=self.send.at[n],
                        recv_sem=self.recv.at[n],
                        device_id=(px + dx, py + dy),
                        device_id_type=MESH,
                    ))
                    n += 1

                @pl.when(inside(sign * dx, sign * dy))
                def _():
                    for copy in copies:
                        act(copy)

        def start(self):
            self.each(lambda c: c.start(), 1)

        def arrive(self):
            self.each(lambda c: c.wait_recv(), -1)

        def sent(self):
            self.each(lambda c: c.wait_send(), 1)

        def unpack(self, ref, ox, oy, change=lambda v: v):
            hx, (bx, by) = self.hx, self.block
            ref[ox - hx : ox, oy : oy + by] = change(self.xland[0])
            ref[ox + bx : ox + bx + hx, oy : oy + by] = change(self.xland[1])
            for yland, (d, w) in zip(self.yland, self.pieces):
                ref[ox - hx : ox + bx + hx, oy - d - w : oy - d] = change(yland[0])
                ref[ox - hx : ox + bx + hx, oy + by + d : oy + by + d + w] = change(yland[1])

    def along(axis, ref, send, recv, base):
        count, me = (py_count, py) if axis else (px_count, px)
        region = ref.at[px, py] if axis else ref.at[px]

        def each(act):
            for k in range(1, count):
                to = lax.rem(me + k, count)
                act(pltpu.make_async_remote_copy(
                    src_ref=region,
                    dst_ref=region,
                    send_sem=send.at[base + k - 1],
                    recv_sem=recv.at[base + k - 1],
                    device_id=(px, to) if axis else (to, py),
                    device_id_type=MESH,
                ))

        def arrive():
            for k in range(1, count):
                frm = lax.rem(me + count - k, count)
                landed = ref.at[px, frm] if axis else ref.at[frm]
                pltpu.make_async_remote_copy(
                    src_ref=landed,
                    dst_ref=landed,
                    send_sem=send.at[base + k - 1],
                    recv_sem=recv.at[base + k - 1],
                    device_id=(px, frm) if axis else (frm, py),
                    device_id_type=MESH,
                ).wait_recv()

        return (lambda: each(lambda c: c.start())), arrive, (lambda: each(lambda c: c.wait_send()))

    m0, f0, u0 = l0[0], l0[5], l0[6]
    m1, f1, u1 = l1[0], l1[5], l1[6]
    own_copies = [
        pltpu.make_async_copy(a, b, copy_sem.at[i])
        for i, (a, b) in enumerate(((density, den), (source, src)))
    ]
    for c in own_copies:
        c.start()
    block0, block1 = (bx, by), (bx1, by1)
    halo_m0 = Halo(halos[0], 3, THREE, block0)
    halo_f0 = Halo(halos[1], 2, TWO, block0)
    halo_u0 = Halo(halos[2], 2, TWO, block0)
    halo_m1 = Halo(halos[3], 3, THREE, block1)
    halo_f1 = Halo(halos[4], 2, TWO, block1)
    halo_u1 = Halo(halos[5], 3, THREE, block1)
    all_halos = (halo_m0, halo_f0, halo_u0, halo_m1, halo_f1, halo_u1)
    for h, value in zip(all_halos, (1.0, 0.0, 0.0, 1.0, 0.0, 0.0)):
        h.fill(value)

    barrier = pltpu.get_barrier_semaphore()
    for k in range(1, py_count):
        pl.semaphore_signal(barrier, 1, device_id=(px, lax.rem(py + k, py_count)), device_id_type=MESH)
    for k in range(1, px_count):
        pl.semaphore_signal(barrier, 1, device_id=(lax.rem(px + k, px_count), py), device_id_type=MESH)
    for dx, dy in DIRECTIONS:
        if dx and dy:
            @pl.when(inside(dx, dy))
            def _():
                pl.semaphore_signal(barrier, 1, device_id=(px + dx, py + dy), device_id_type=MESH)
    beside_x = jnp.minimum(px, 1) + jnp.minimum(px_count - 1 - px, 1)
    beside_y = jnp.minimum(py, 1) + jnp.minimum(py_count - 1 - py, 1)
    own_copies[0].wait()
    halo_m0.pack(den, 0, 0)
    pl.semaphore_wait(barrier, px_count + py_count - 2 + beside_x * beside_y)

    halo_m0.start()
    own_copies[1].wait()
    halo_f0.pack(src, 0, 0)
    halo_f0.start()

    r_fine = matrix((nz, LANES), lambda z, c: z // 2 == c, 0.125)
    r_low = matrix((LANES, LANES), lambda z, c: z // 2 == c, 0.125)
    r_high = matrix((LANES, LANES), lambda z, c: z // 2 + LANES // 2 == c, 0.125)
    half = LANES // 2
    r_pack = matrix(
        (LANES, LANES), lambda z, c: (z // half == c // half) & ((z % half) // 2 == c % half), 0.125
    )

    def restrict0(get, dst):
        def body(i, n):
            pair_slabs(tmp, i, get(HX0 + 2 * i, 2 * n))

        chunks(0, bx1, 2 * (y0 // ROWS) * (nz // LANES), 24, body)
        value = dot(pair_rows(tmp, bx1, by1, nz).reshape(bx1 * by1, nz), r_fine)
        dst[HX1 : HX1 + bx1, ROWS : ROWS + by1] = value.reshape(bx1, by1, LANES)

    def restrict1(get, dst):
        def body(i, n):
            pair_slabs(tmp, i, get(HX1 + 2 * i, 2 * n))

        chunks(0, bx2, 2 * (y1 // ROWS), 24, body)
        sums = pair_rows(tmp, bx2, by2, LANES)
        for i in range(bx2):
            t1[i * by2 : (i + 1) * by2] = sums[i]
        n = bx2 * by2 // 2
        dst[px, py] = dot(t1[0:n], r_low) + dot(t1[n : 2 * n], r_high)

    wide0, wide1, wide2, wide3 = (l[0].shape[0] for l in (l0, l1, l2, l3))
    y0, y1 = l0[0].shape[1], l1[0].shape[1]

    def own(x, n):
        m0[pl.ds(HX0 + x, n), HY0 : HY0 + by] = 1.0 / den[pl.ds(x, n)]
        f0[pl.ds(HX0 + x, n), HY0 : HY0 + by] = src[pl.ds(x, n)]

    chunks(0, bx, (by // ROWS) * (nz // LANES), 24, own)
    restrict0(lambda x, n: m0[pl.ds(x, n), HY0 : HY0 + by], m1)
    halo_m1.pack(m1, HX1, ROWS)
    halo_m1.start()
    restrict1(lambda x, n: m1[pl.ds(x, n), ROWS : ROWS + by1], gm)
    ma_start, ma_arrive, ma_sent = along(1, gm, sa, ra, 0)
    fa_start, fa_arrive, fa_sent = along(1, gf, sa, ra, py_count - 1)
    mb_start, mb_arrive, mb_sent = along(0, gm, sb, rb, 0)
    fb_start, fb_arrive, fb_sent = along(0, gf, sb, rb, px_count - 1)
    ma_start()

    level0 = Level(l0, 1.0, px * bx - HX0, nx, (py * by - HY0, ny), (nz, nz), (HX0 - 2, HX0 + bx + 2), False)
    level1 = Level(l1, 0.25, px * bx1 - HX1, nx // 2, (py * by1 - ROWS, ny // 2),
                   (nz // 2, LANES), (HX1 - 2, HX1 + bx1 + 2), False)
    level2 = Level(l2, 0.25**2, -PAD2, nx // 4, (0, ny // 4), (nz // 4, half),
                   (PAD2, wide2 - PAD2), True)
    level3 = Level(l3, 0.25**3, -1, nx // 8, (0, ny // 8), (nz // 8, half), (1, wide3 - 1), True)
    level2.clear(level2.g, level2.u)
    level3.clear(level3.g, level3.u)

    halo_m0.arrive()
    halo_m0.unpack(m0, HX0, HY0, lambda v: 1.0 / v)
    level0.setup()
    halo_f0.arrive()
    halo_f0.unpack(f0, HX0, HY0)
    level0.scale()
    level0.sweep(f0, u0, 1)
    restrict0(lambda x, n: level0.residual(x, n)[:, HY0 : HY0 + by], f1)
    halo_f1.pack(f1, HX1, ROWS)
    halo_f1.start()
    halo_u0.pack(u0, HX0, HY0)
    halo_u0.start()

    ma_arrive()
    mb_start()
    halo_m1.arrive()
    halo_m1.unpack(m1, HX1, ROWS)
    level1.setup()
    halo_f1.arrive()
    halo_f1.unpack(f1, HX1, ROWS)
    level1.scale()
    level1.sweep(f1, u1, 1)
    restrict1(lambda x, n: level1.residual(x, n)[:, ROWS : ROWS + by1], gf)
    fa_start()
    halo_u1.pack(u1, HX1, ROWS)
    halo_u1.start()

    def spread(gathered, dst):
        n = bx2 // 2
        lane = iota((n * by2, LANES), 1)
        groups = py_count // 2

        def body(p):
            for q in range(groups):
                a, b = gathered[p, q], gathered[p, q + groups]
                first = jnp.where(lane < half, a, pltpu.roll(b, half, 1))
                second = jnp.where(lane < half, pltpu.roll(a, half, 1), b)
                for i in range(n):
                    rows = slice(q * by2, (q + 1) * by2)
                    piece = slice(i * by2, (i + 1) * by2)
                    dst[PAD2 + p * bx2 + i, rows] = first[piece]
                    dst[PAD2 + p * bx2 + n + i, rows] = second[piece]

        loop(0, px_count, body)

    def pair2(get, dst):
        count = wide3 - 2
        rows = l3[0].shape[1]

        def body(i, n):
            pair_slabs(tmp, i, get(PAD2 + 2 * i, 2 * n))

        chunks(0, count, 2 * level2.size, 24, body)
        sums = pair_rows(tmp, count, rows, LANES)
        dst[1 : 1 + count] = dot(sums.reshape(count * rows, LANES), r_pack).reshape(
            count, rows, LANES
        )

    mb_arrive()
    one2 = jnp.ones((PAD2,) + level2.shape, jnp.float32)
    one3 = jnp.ones(level3.shape, jnp.float32)
    m2, m3 = l2[0], l3[0]
    spread(gm, m2)
    m2[0:PAD2] = one2
    m2[wide2 - PAD2 :] = one2
    level2.setup()
    pair2(lambda x, n: m2[pl.ds(x, n)], m3)
    m3[0] = one3
    m3[wide3 - 1] = one3

    inner3 = slice(1, wide3 - 1)
    m3[inner3] = jnp.where(level3.gz < level3.nz, m3[inner3], 1.0)
    level3.setup()

    fa_arrive()
    fb_start()
    fb_arrive()
    f2, f3 = l2[5], l3[5]
    spread(gf, f2)

    level2.scale()
    level2.sweep(level2.g, level2.u)
    pair2(level2.residual, f3)

    level3.scale()
    m3[0] = jnp.zeros(level3.shape, jnp.float32)
    m3[wide3 - 1] = jnp.zeros(level3.shape, jnp.float32)
    level3.sweep(f3, level3.u)
    now, later = level3.u, m3
    for _ in range(COARSE - 2):
        level3.sweep(now, later)
        now, later = later, now

    p_pack = matrix(
        (LANES, LANES), lambda k, z: (z // half == k // half) & ((z % half) // 2 == k % half), 1.0
    )
    count3, rows3 = wide3 - 2, l3[0].shape[1]
    e3 = dot(now[1 : 1 + count3].reshape(count3 * rows3, LANES), p_pack)
    add_double(tmp, e3.reshape(count3, rows3, LANES), level2.u, PAD2, level2.size)
    zero2 = jnp.zeros((PAD2,) + level2.shape, jnp.float32)
    m2[0:PAD2] = zero2
    m2[wide2 - PAD2 :] = zero2
    level2.u[0:PAD2] = zero2
    level2.u[wide2 - PAD2 :] = zero2
    level2.sweep(level2.u, m2)
    level2.sweep(m2, level2.u)

    full = 2 * level2.shape[0]
    shift = lax.rem(full + ROWS // 2 - py * by2, full)
    take = pe1.shape[1]

    halo_u1.arrive()
    halo_u1.unpack(u1, HX1, ROWS)

    def fetch(c, n):
        e = [level2.u[px * bx2 + c + j] for j in range(n)]
        e = [jnp.concatenate([one, pltpu.roll(one, half, 1)], 0) for one in e]
        e = [pltpu.roll(one, shift, 0)[0:take] for one in e]
        for j in range(n):
            pe1[c + j] = e[j]

    chunks(0, wide1 // 2, 2 * level2.size, 32, fetch)
    p_one = matrix((LANES, LANES), lambda k, z: z // 2 == k, 1.0)
    e2 = dot(pe1[...].reshape(-1, LANES), p_one).reshape(pe1.shape)
    add_double(tmp, e2[:, 0 : y1 // 2], level1.u, 0, level1.size)
    level1.sweep(u1, m1)
    level1.sweep(m1, u1, 1)

    p_zero = matrix((LANES, nz), lambda k, z: z // 2 == k, 1.0)
    base = HX1 - HX0 // 2
    count = wide0 // 2
    e1 = dot(level1.u[base : base + count].reshape(count * y1, LANES), p_zero)
    pe0[...] = e1.reshape(pe0.shape)
    low = ROWS - HY0 // 2
    halo_u0.arrive()
    halo_u0.unpack(u0, HX0, HY0)
    add_double(tmp, pe0[:, low : low + y0 // 2], level0.u, 0, level0.size)
    level0.sweep(u0, m0, 1)

    def last(x, n):
        v, rest = level0.change(m0, HX0 + x, n)
        out[pl.ds(x, n)] = (0.2 * v + rest)[:, HY0 : HY0 + by]

    chunks(0, bx, level0.size, 24, last)

    for h in all_halos:
        h.sent()
    for done in (ma_sent, mb_sent, fa_sent, fb_sent):
        done()


def per_device(px_count, py_count, source, density):
    bx, by, nz = source.shape
    f32 = jnp.float32
    bx1, by1, bx2, by2 = bx // 2, by // 2, bx // 4, by // 4

    def level(wide, rows, lanes):
        return [pltpu.VMEM((wide, rows, lanes), f32)] * 7

    y0, y1 = by + 2 * HY0, by1 + 2 * ROWS
    wide0, wide1 = bx + 2 * HX0, bx1 + 2 * HX1
    x2, rows2 = bx2 * px_count, by2 * py_count // 2
    ext = pltpu.VMEM(source.shape, f32)

    def halo(hx, pieces, rows, cols, lanes):
        copies = pltpu.SemaphoreType.DMA((2 + 6 * len(pieces),))
        return [
            pltpu.VMEM((2, hx, cols, lanes), f32),
            pltpu.VMEM((2, hx, cols, lanes), f32),
            [pltpu.VMEM((2, rows, w, lanes), f32) for _, w in pieces],
            [pltpu.VMEM((2, rows + 2 * hx, w, lanes), f32) for _, w in pieces],
            copies,
            copies,
        ]

    take = -(-(y1 // 2) // ROWS) * ROWS
    gather = pltpu.VMEM((px_count, py_count, bx2 * by2 // 2, LANES), f32)
    scratch = [
        ext,
        ext,
        level(wide0, y0, nz),
        level(wide1, y1, LANES),
        level(x2 + 2 * PAD2, rows2, LANES),
        level(x2 // 2 + 2, rows2 // 2, LANES),
        pltpu.VMEM((wide0 // 2, y1, nz), f32),
        pltpu.VMEM((wide1 // 2, take, LANES), f32),
        pltpu.VMEM((bx2 * by2, LANES), f32),
        pltpu.VMEM((nz // LANES, max(wide0, wide1, x2) // 2, max(y0, y1, rows2), LANES), f32),
        gather,
        gather,
        pltpu.SemaphoreType.DMA((2,)),
        [
            halo(3, THREE, bx, by, nz),
            halo(2, TWO, bx, by, nz),
            halo(2, TWO, bx, by, nz),
            halo(3, THREE, bx1, by1, LANES),
            halo(2, TWO, bx1, by1, LANES),
            halo(3, THREE, bx1, by1, LANES),
        ],
        pltpu.SemaphoreType.DMA((2 * (py_count - 1),)),
        pltpu.SemaphoreType.DMA((2 * (py_count - 1),)),
        pltpu.SemaphoreType.DMA((2 * (px_count - 1),)),
        pltpu.SemaphoreType.DMA((2 * (px_count - 1),)),
    ]
    return pl.pallas_call(
        functools.partial(kernel, (px_count, py_count)),
        out_shape=jax.ShapeDtypeStruct(source.shape, f32),
        in_specs=[pl.BlockSpec(memory_space=pl.ANY)] * 2,
        out_specs=pl.BlockSpec(memory_space=pltpu.VMEM),
        scratch_shapes=scratch,
        compiler_params=pltpu.CompilerParams(
            collective_id=0, has_side_effects=True, vmem_limit_bytes=56 * 1024 * 1024
        ),
    )(source, density)


def solution(mesh):
    spec = P("px", "py", None)
    return jax.shard_map(
        functools.partial(per_device, mesh.shape["px"], mesh.shape["py"]),
        mesh=mesh,
        in_specs=(spec, spec),
        out_specs=spec,
        check_vma=False,
    )
```

```python
import functools

import jax
import jax.numpy as jnp
from jax import lax
from jax.experimental import pallas as pl
from jax.experimental.pallas import tpu as pltpu
from jax.sharding import PartitionSpec as P

COARSE = 8
LANES = 128
HX0, HX1, HY, PAD2 = 4, 4, 4, 2
THREE, TWO = ((0, 2), (2, 1)), ((0, 2),)
ROWS = 8
DIRECTIONS = [(dx, dy) for dx in (-1, 0, 1) for dy in (-1, 0, 1) if (dx, dy) != (0, 0)]
MESH = pl.DeviceIdType.MESH


def iota(shape, dim):
    return lax.broadcasted_iota(jnp.int32, shape, dim)


def dot(a, b):
    return jnp.dot(a, b, precision=lax.Precision.HIGHEST, preferred_element_type=jnp.float32)


def matrix(shape, test, value):
    return jnp.where(test(iota(shape, 0), iota(shape, 1)), value, 0.0).astype(jnp.float32)


def loop(low, high, body, unroll=1):
    def step(i, carry):
        body(i)
        return carry

    lax.fori_loop(low, high, step, 0, unroll=unroll)


def chunks(low, high, size, most, body):
    count = high - low
    n = max(d for d in range(1, count + 1) if count % d == 0 and (d == 1 or d * size <= most))
    if n == count:
        body(low, n)
    else:
        loop(0, count // n, lambda i: body(low + i * n, n))


class Level:
    def __init__(self, refs, factor, start, total, rows, lanes, span, packed):
        (self.m, self.wx, self.wy, self.wz, self.k, self.g, self.u) = refs
        self.low, self.high = span
        self.half = 0.5 * factor
        self.start, self.total = start, total
        shape = self.m.shape[1:]
        self.shape, self.packed = shape, packed
        row, lane = iota(shape, 0), iota(shape, 1)
        first, total_y = rows
        nz, stride = lanes
        group = lane // stride if packed else 0
        gy = row + group * shape[0]
        if not packed:
            gy = first + jnp.where(row < shape[0] - HY, row, row - shape[0])
        gz = lane % stride if packed else lane
        self.row = row
        self.size = -(-shape[0] // ROWS) * (shape[1] // LANES)

        def keep(pos, count, span):
            plus = (pos != count - 1) & (pos != -1) & (pos != span - 1)
            minus = (pos != 0) & (pos != count)
            return jnp.where(plus, 1.0, 0.0), jnp.where(minus, 1.0, 0.0)

        self.kyp, self.kym = keep(gy, total_y, -9)
        self.kzp, self.kzm = keep(gz, nz, stride)
        self.gz, self.nz = gz, nz

    def y_minus(self, t):
        r = pltpu.roll(t, 1, t.ndim - 2)
        if self.packed:
            r = jnp.where(self.row == 0, pltpu.roll(r, LANES // 2, r.ndim - 1), r)
        return r

    def y_plus(self, t):
        r = pltpu.roll(t, self.shape[0] - 1, t.ndim - 2)
        if self.packed:
            r = jnp.where(self.row == self.shape[0] - 1, pltpu.roll(r, LANES // 2, r.ndim - 1), r)
        return r

    def z_minus(self, t):
        return pltpu.roll(t, 1, t.ndim - 1)

    def z_plus(self, t):
        return pltpu.roll(t, self.shape[1] - 1, t.ndim - 1)

    def clear(self, *refs):
        for i in (self.low - 1, self.high):
            for ref in refs:
                ref[i] = jnp.zeros(self.shape, jnp.float32)

    def face(self, x):
        gx = self.start + x
        return jnp.where((gx != self.total - 1) & (gx != -1), 1.0, 0.0)

    def setup(self, source=None):
        before = self.low - 1
        self.wx[before] = (self.half * self.face(before)) * (self.m[before] + self.m[self.low])
        known = self.kyp + self.kym + self.kzp + self.kzm

        def body(x, n):
            m = [self.m[x - 1 + j] for j in range(n + 2)]
            f = None if source is None else [source(x + j) for j in range(n)]
            k = [self.face(x - 1 + j) for j in range(n + 1)]
            s = [k[j] * (m[j] + m[j + 1]) for j in range(n + 1)]
            done = []
            for j in range(n):
                c = m[j + 1]
                wyp = self.kyp * (c + self.y_plus(c))
                wym = self.kym * (c + self.y_minus(c))
                wzp = self.kzp * (c + self.z_plus(c))
                wzm = self.kzm * (c + self.z_minus(c))
                missing = 6.0 - (k[j] + k[j + 1]) - known
                diag = ((s[j] + s[j + 1]) + (wyp + wym)) + ((wzp + wzm) + 2.0 * c * missing)
                done.append((self.half * s[j + 1], self.half * wyp, self.half * wzp,
                             0.8 / (self.half * diag)))
            for j, (wx, wy, wz, inverse) in enumerate(done):
                self.wx[x + j] = wx
                self.wy[x + j] = wy
                self.wz[x + j] = wz
                self.k[x + j] = inverse
                if f is not None:
                    self.g[x + j] = inverse * f[j]

        chunks(self.low, self.high, self.size, 12, body)

    def scale(self):
        def body(x, n):
            at = pl.ds(x, n)
            self.g[at] = self.k[at] * self.g[at]

        chunks(self.low, self.high, self.size, 24, body)

    def change(self, ref, x, n):
        at = pl.ds(x, n)
        v, wy, wz = ref[at], self.wy[at], self.wz[at]
        total = self.wx[at] * ref[pl.ds(x + 1, n)] + self.wx[pl.ds(x - 1, n)] * ref[pl.ds(x - 1, n)]
        total = total + (wy * self.y_plus(v) + self.y_minus(wy * v))
        total = total + (wz * self.z_plus(v) + self.z_minus(wz * v))
        return v, self.g[at] + self.k[at] * total

    def sweep(self, src, dst, inset=0):
        def body(x, n):
            v, rest = self.change(src, x, n)
            dst[pl.ds(x, n)] = 0.2 * v + rest

        chunks(self.low + inset, self.high - inset, self.size, 24, body)

    def residual(self, x, n):
        v, rest = self.change(self.u, x, n)
        return (rest - 0.8 * v) / self.k[pl.ds(x, n)]


def columns(width):
    return [slice(c, c + LANES) for c in range(0, width, LANES)]


def pair_slabs(tmp, i, value):
    count, rows, width = value.shape
    sums = [value[j] + value[j + 1] for j in range(0, count, 2)]
    for j, both in enumerate(sums):
        for k, c in enumerate(columns(width)):
            tmp[k, i + j, 0:rows] = both[:, c]


def pair_rows(tmp, count, rows, width):
    parts = [
        tmp[k, 0:count, pl.ds(0, rows, stride=2)] + tmp[k, 0:count, pl.ds(1, rows, stride=2)]
        for k in range(width // LANES)
    ]
    return parts[0] if len(parts) == 1 else jnp.concatenate(parts, 2)


def add_double(tmp, values, target, first, size):
    rows = 0
    for value in values:
        count, more, width = value.shape
        for k, c in enumerate(columns(width)):
            tmp[k, 0:count, pl.ds(2 * rows, more, stride=2)] = value[:, :, c]
            tmp[k, 0:count, pl.ds(2 * rows + 1, more, stride=2)] = value[:, :, c]
        rows += more

    def body(i, n):
        parts = [tmp[k, pl.ds(i, n), 0 : 2 * rows] for k in range(width // LANES)]
        e = parts[0] if len(parts) == 1 else jnp.concatenate(parts, 2)
        old = target[pl.ds(first + 2 * i, 2 * n)]
        new = [old[j] + e[j // 2] for j in range(2 * n)]
        for j in range(2 * n):
            target[first + 2 * i + j] = new[j]

    chunks(0, count, 2 * size, 24, body)


def kernel(sizes, source, density, out, den, src, l0, l1, l2, l3, pe0, pe1, t1, tmp,
           gm, gf, copy_sem, halos, sa, ra, sb, rb):
    px_count, py_count = sizes
    px, py = lax.axis_index("px"), lax.axis_index("py")
    bx, by, nz = source.shape
    nx, ny = bx * px_count, by * py_count
    bx1, by1, bx2, by2 = bx // 2, by // 2, bx // 4, by // 4

    def inside(dx, dy):
        test = None
        for d, pos, count in ((dx, px, px_count), (dy, py, py_count)):
            if d:
                one = (pos < count - 1) if d > 0 else (pos > 0)
                test = one if test is None else test & one
        return test

    class Halo:
        def __init__(self, refs, hx, pieces, block):
            self.xsend, self.xland, self.ysend, self.yland, self.send, self.recv = refs
            self.hx, self.pieces, self.block = hx, pieces, block

        def fill(self, value):
            edges = ((px == 0, 0, 0), (px == px_count - 1, 0, 1),
                     (py == 0, 1, 0), (py == py_count - 1, 1, 1))
            hx, bx = self.hx, self.block[0]
            for test, dim, side in edges:
                @pl.when(test)
                def _():
                    if dim == 0:
                        ref = self.xland
                        ref[side] = jnp.full(ref.shape[1:], value, jnp.float32)
                    for ref in self.yland:
                        if dim:
                            ref[side] = jnp.full(ref.shape[1:], value, jnp.float32)
                        else:
                            at = side * (hx + bx)
                            for s in range(2):
                                ref[s, at : at + hx] = jnp.full((hx,) + ref.shape[2:], value, jnp.float32)

        def pack(self, ref, ox):
            hx, (bx, by) = self.hx, self.block
            self.xsend[0] = ref[ox : ox + hx, 0:by]
            self.xsend[1] = ref[ox + bx - hx : ox + bx, 0:by]
            for ysend, (d, w) in zip(self.ysend, self.pieces):
                ysend[0] = ref[ox : ox + bx, d : d + w]
                ysend[1] = ref[ox : ox + bx, by - d - w : by - d]

        def each(self, act, sign):
            hx, bx = self.hx, self.block[0]
            n = 0
            for dx, dy in DIRECTIONS:
                if dy == 0:
                    side = (dx + 1) // 2
                    pairs = [(self.xsend.at[side], self.xland.at[1 - side])]
                else:
                    side = (dy + 1) // 2
                    own, there, count = ((0, hx + bx, hx), (0, hx, bx), (bx - hx, 0, hx))[dx + 1]
                    pairs = [
                        (a.at[side, pl.ds(own, count)], b.at[1 - side, pl.ds(there, count)])
                        for a, b in zip(self.ysend, self.yland)
                    ]
                copies = []
                for a, b in pairs:
                    copies.append(pltpu.make_async_remote_copy(
                        src_ref=a,
                        dst_ref=b,
                        send_sem=self.send.at[n],
                        recv_sem=self.recv.at[n],
                        device_id=(px + dx, py + dy),
                        device_id_type=MESH,
                    ))
                    n += 1

                @pl.when(inside(sign * dx, sign * dy))
                def _():
                    for copy in copies:
                        act(copy)

        def start(self):
            self.each(lambda c: c.start(), 1)

        def arrive(self):
            self.each(lambda c: c.wait_recv(), -1)

        def sent(self):
            self.each(lambda c: c.wait_send(), 1)

        def unpack(self, ref, ox, change=lambda v: v):
            hx, (bx, by), rows = self.hx, self.block, ref.shape[1]
            ref[ox - hx : ox, 0:by] = change(self.xland[0])
            ref[ox + bx : ox + bx + hx, 0:by] = change(self.xland[1])
            for yland, (d, w) in zip(self.yland, self.pieces):
                ref[ox - hx : ox + bx + hx, rows - d - w : rows - d] = change(yland[0])
                ref[ox - hx : ox + bx + hx, by + d : by + d + w] = change(yland[1])

    def along(axis, ref, send, recv, base):
        count, me = (py_count, py) if axis else (px_count, px)
        region = ref.at[px, py] if axis else ref.at[px]

        def each(act):
            for k in range(1, count):
                to = lax.rem(me + k, count)
                act(pltpu.make_async_remote_copy(
                    src_ref=region,
                    dst_ref=region,
                    send_sem=send.at[base + k - 1],
                    recv_sem=recv.at[base + k - 1],
                    device_id=(px, to) if axis else (to, py),
                    device_id_type=MESH,
                ))

        def arrive():
            for k in range(1, count):
                frm = lax.rem(me + count - k, count)
                landed = ref.at[px, frm] if axis else ref.at[frm]
                pltpu.make_async_remote_copy(
                    src_ref=landed,
                    dst_ref=landed,
                    send_sem=send.at[base + k - 1],
                    recv_sem=recv.at[base + k - 1],
                    device_id=(px, frm) if axis else (frm, py),
                    device_id_type=MESH,
                ).wait_recv()

        return (lambda: each(lambda c: c.start())), arrive, (lambda: each(lambda c: c.wait_send()))

    m0, f0, u0 = l0[0], l0[5], l0[6]
    m1, f1, u1 = l1[0], l1[5], l1[6]
    own_copies = [
        pltpu.make_async_copy(a, b, copy_sem.at[i])
        for i, (a, b) in enumerate(((density, den), (source, src)))
    ]
    for c in own_copies:
        c.start()
    block0, block1 = (bx, by), (bx1, by1)
    halo_m0 = Halo(halos[0], 3, THREE, block0)
    halo_f0 = Halo(halos[1], 2, TWO, block0)
    halo_u0 = Halo(halos[2], 2, TWO, block0)
    halo_m1 = Halo(halos[3], 3, THREE, block1)
    halo_f1 = Halo(halos[4], 2, TWO, block1)
    halo_u1 = Halo(halos[5], 3, THREE, block1)
    all_halos = (halo_m0, halo_f0, halo_u0, halo_m1, halo_f1, halo_u1)
    for h, value in zip(all_halos, (1.0, 0.0, 0.0, 1.0, 0.0, 0.0)):
        h.fill(value)

    barrier = pltpu.get_barrier_semaphore()
    for k in range(1, py_count):
        pl.semaphore_signal(barrier, 1, device_id=(px, lax.rem(py + k, py_count)), device_id_type=MESH)
    for k in range(1, px_count):
        pl.semaphore_signal(barrier, 1, device_id=(lax.rem(px + k, px_count), py), device_id_type=MESH)
    for dx, dy in DIRECTIONS:
        if dx and dy:
            @pl.when(inside(dx, dy))
            def _():
                pl.semaphore_signal(barrier, 1, device_id=(px + dx, py + dy), device_id_type=MESH)
    beside_x = jnp.minimum(px, 1) + jnp.minimum(px_count - 1 - px, 1)
    beside_y = jnp.minimum(py, 1) + jnp.minimum(py_count - 1 - py, 1)
    own_copies[0].wait()
    halo_m0.pack(den, 0)
    pl.semaphore_wait(barrier, px_count + py_count - 2 + beside_x * beside_y)

    halo_m0.start()
    own_copies[1].wait()
    halo_f0.pack(src, 0)
    halo_f0.start()

    r_fine = matrix((nz, LANES), lambda z, c: z // 2 == c, 0.125)
    r_low = matrix((LANES, LANES), lambda z, c: z // 2 == c, 0.125)
    r_high = matrix((LANES, LANES), lambda z, c: z // 2 + LANES // 2 == c, 0.125)
    half = LANES // 2
    r_pack = matrix(
        (LANES, LANES), lambda z, c: (z // half == c // half) & ((z % half) // 2 == c % half), 0.125
    )

    def restrict0(get, dst):
        def body(i, n):
            pair_slabs(tmp, i, get(HX0 + 2 * i, 2 * n))

        chunks(0, bx1, 2 * (y0 // ROWS) * (nz // LANES), 24, body)
        value = dot(pair_rows(tmp, bx1, by1, nz).reshape(bx1 * by1, nz), r_fine)
        dst[HX1 : HX1 + bx1, 0:by1] = value.reshape(bx1, by1, LANES)

    def restrict1(get, dst):
        def body(i, n):
            pair_slabs(tmp, i, get(HX1 + 2 * i, 2 * n))

        chunks(0, bx2, 2 * (y1 // ROWS), 24, body)
        sums = pair_rows(tmp, bx2, by2, LANES)
        for i in range(bx2):
            t1[i * by2 : (i + 1) * by2] = sums[i]
        n = bx2 * by2 // 2
        dst[px, py] = dot(t1[0:n], r_low) + dot(t1[n : 2 * n], r_high)

    wide0, wide1, wide2, wide3 = (l[0].shape[0] for l in (l0, l1, l2, l3))
    y0, y1 = l0[0].shape[1], l1[0].shape[1]

    def own(x, n):
        m0[pl.ds(HX0 + x, n), 0:by] = 1.0 / den[pl.ds(x, n)]
        f0[pl.ds(HX0 + x, n), 0:by] = src[pl.ds(x, n)]

    chunks(0, bx, (by // ROWS) * (nz // LANES), 24, own)
    restrict0(lambda x, n: m0[pl.ds(x, n), 0:by], m1)
    halo_m1.pack(m1, HX1)
    halo_m1.start()
    restrict1(lambda x, n: m1[pl.ds(x, n), 0:by1], gm)
    ma_start, ma_arrive, ma_sent = along(1, gm, sa, ra, 0)
    fa_start, fa_arrive, fa_sent = along(1, gf, sa, ra, py_count - 1)
    mb_start, mb_arrive, mb_sent = along(0, gm, sb, rb, 0)
    fb_start, fb_arrive, fb_sent = along(0, gf, sb, rb, px_count - 1)
    ma_start()

    level0 = Level(l0, 1.0, px * bx - HX0, nx, (py * by, ny), (nz, nz), (HX0 - 2, HX0 + bx + 2), False)
    level1 = Level(l1, 0.25, px * bx1 - HX1, nx // 2, (py * by1, ny // 2),
                   (nz // 2, LANES), (HX1 - 2, HX1 + bx1 + 2), False)
    level2 = Level(l2, 0.25**2, -PAD2, nx // 4, (0, ny // 4), (nz // 4, half),
                   (PAD2, wide2 - PAD2), True)
    level3 = Level(l3, 0.25**3, -1, nx // 8, (0, ny // 8), (nz // 8, half), (1, wide3 - 1), True)
    level2.clear(level2.g, level2.u)
    level3.clear(level3.g, level3.u)

    halo_m0.arrive()
    halo_m0.unpack(m0, HX0, lambda v: 1.0 / v)
    level0.setup()
    halo_f0.arrive()
    halo_f0.unpack(f0, HX0)
    ma_arrive()
    mb_start()
    level0.scale()
    level0.sweep(f0, u0, 1)
    restrict0(lambda x, n: level0.residual(x, n)[:, 0:by], f1)
    halo_f1.pack(f1, HX1)
    halo_f1.start()
    halo_u0.pack(u0, HX0)

    halo_m1.arrive()
    halo_m1.unpack(m1, HX1)
    level1.setup()
    halo_f1.arrive()
    halo_f1.unpack(f1, HX1)
    level1.scale()
    level1.sweep(f1, u1, 1)
    restrict1(lambda x, n: level1.residual(x, n)[:, 0:by1], gf)
    fa_start()
    halo_u1.pack(u1, HX1)

    def spread(gathered, dst):
        n = bx2 // 2
        lane = iota((n * by2, LANES), 1)
        groups = py_count // 2

        def body(p):
            for q in range(groups):
                a, b = gathered[p, q], gathered[p, q + groups]
                first = jnp.where(lane < half, a, pltpu.roll(b, half, 1))
                second = jnp.where(lane < half, pltpu.roll(a, half, 1), b)
                for i in range(n):
                    rows = slice(q * by2, (q + 1) * by2)
                    piece = slice(i * by2, (i + 1) * by2)
                    dst[PAD2 + p * bx2 + i, rows] = first[piece]
                    dst[PAD2 + p * bx2 + n + i, rows] = second[piece]

        loop(0, px_count, body)

    def pair2(get, dst):
        count = wide3 - 2
        rows = l3[0].shape[1]

        def body(i, n):
            pair_slabs(tmp, i, get(PAD2 + 2 * i, 2 * n))

        chunks(0, count, 2 * level2.size, 24, body)
        sums = pair_rows(tmp, count, rows, LANES)
        dst[1 : 1 + count] = dot(sums.reshape(count * rows, LANES), r_pack).reshape(
            count, rows, LANES
        )

    mb_arrive()
    one2 = jnp.ones((PAD2,) + level2.shape, jnp.float32)
    one3 = jnp.ones(level3.shape, jnp.float32)
    m2, m3 = l2[0], l3[0]
    spread(gm, m2)
    m2[0:PAD2] = one2
    m2[wide2 - PAD2 :] = one2
    level2.setup()
    pair2(lambda x, n: m2[pl.ds(x, n)], m3)
    m3[0] = one3
    m3[wide3 - 1] = one3

    inner3 = slice(1, wide3 - 1)
    m3[inner3] = jnp.where(level3.gz < level3.nz, m3[inner3], 1.0)
    level3.setup()

    fa_arrive()
    fb_start()
    halo_u1.start()
    halo_u0.start()
    fb_arrive()
    f2, f3 = l2[5], l3[5]
    spread(gf, f2)

    level2.scale()
    level2.sweep(level2.g, level2.u)
    pair2(level2.residual, f3)

    level3.scale()
    m3[0] = jnp.zeros(level3.shape, jnp.float32)
    m3[wide3 - 1] = jnp.zeros(level3.shape, jnp.float32)
    level3.sweep(f3, level3.u)
    now, later = level3.u, m3
    for _ in range(COARSE - 2):
        level3.sweep(now, later)
        now, later = later, now

    p_pack = matrix(
        (LANES, LANES), lambda k, z: (z // half == k // half) & ((z % half) // 2 == k % half), 1.0
    )
    count3, rows3 = wide3 - 2, l3[0].shape[1]
    e3 = dot(now[1 : 1 + count3].reshape(count3 * rows3, LANES), p_pack)
    add_double(tmp, [e3.reshape(count3, rows3, LANES)], level2.u, PAD2, level2.size)
    zero2 = jnp.zeros((PAD2,) + level2.shape, jnp.float32)
    m2[0:PAD2] = zero2
    m2[wide2 - PAD2 :] = zero2
    level2.u[0:PAD2] = zero2
    level2.u[wide2 - PAD2 :] = zero2
    level2.sweep(level2.u, m2)
    level2.sweep(m2, level2.u)

    full = 2 * level2.shape[0]
    shift = lax.rem(full - py * by2, full)
    near = by2 + HY // 2

    halo_u1.arrive()
    halo_u1.unpack(u1, HX1)

    def fetch(c, n):
        e = [level2.u[px * bx2 + c + j] for j in range(n)]
        e = [jnp.concatenate([one, pltpu.roll(one, half, 1)], 0) for one in e]
        e = [pltpu.roll(one, shift, 0) for one in e]
        for j in range(n):
            pe1[c + j, 0:near] = e[j][0:near]
            pe1[c + j, near : near + HY // 2] = e[j][full - HY // 2 : full]

    chunks(0, wide1 // 2, 2 * level2.size, 32, fetch)
    p_one = matrix((LANES, LANES), lambda k, z: z // 2 == k, 1.0)
    e2 = dot(pe1[...].reshape(-1, LANES), p_one).reshape(pe1.shape)
    add_double(tmp, [e2[:, 0 : y1 // 2]], level1.u, 0, level1.size)
    level1.sweep(u1, m1)
    level1.sweep(m1, u1, 1)

    p_zero = matrix((LANES, nz), lambda k, z: z // 2 == k, 1.0)
    base = HX1 - HX0 // 2
    count = wide0 // 2
    e1 = dot(level1.u[base : base + count].reshape(count * y1, LANES), p_zero)
    pe0[...] = e1.reshape(pe0.shape)
    halo_u0.arrive()
    halo_u0.unpack(u0, HX0)
    parts = [pe0[:, 0 : by1 + HY // 2], pe0[:, y1 - HY // 2 : y1]]
    add_double(tmp, parts, level0.u, 0, level0.size)
    level0.sweep(u0, m0, 1)

    def last(x, n):
        v, rest = level0.change(m0, HX0 + x, n)
        out[pl.ds(x, n)] = (0.2 * v + rest)[:, 0:by]

    chunks(0, bx, level0.size, 24, last)

    for h in all_halos:
        h.sent()
    for done in (ma_sent, mb_sent, fa_sent, fb_sent):
        done()


def per_device(px_count, py_count, source, density):
    bx, by, nz = source.shape
    f32 = jnp.float32
    bx1, by1, bx2, by2 = bx // 2, by // 2, bx // 4, by // 4

    def level(wide, rows, lanes):
        return [pltpu.VMEM((wide, rows, lanes), f32)] * 7

    y0, y1 = by + 2 * HY, by1 + 2 * HY
    wide0, wide1 = bx + 2 * HX0, bx1 + 2 * HX1
    x2, rows2 = bx2 * px_count, by2 * py_count // 2
    ext = pltpu.VMEM(source.shape, f32)

    def halo(hx, pieces, rows, cols, lanes):
        copies = pltpu.SemaphoreType.DMA((2 + 6 * len(pieces),))
        return [
            pltpu.VMEM((2, hx, cols, lanes), f32),
            pltpu.VMEM((2, hx, cols, lanes), f32),
            [pltpu.VMEM((2, rows, w, lanes), f32) for _, w in pieces],
            [pltpu.VMEM((2, rows + 2 * hx, w, lanes), f32) for _, w in pieces],
            copies,
            copies,
        ]

    take = -(-(y1 // 2) // ROWS) * ROWS
    gather = pltpu.VMEM((px_count, py_count, bx2 * by2 // 2, LANES), f32)
    scratch = [
        ext,
        ext,
        level(wide0, y0, nz),
        level(wide1, y1, LANES),
        level(x2 + 2 * PAD2, rows2, LANES),
        level(x2 // 2 + 2, rows2 // 2, LANES),
        pltpu.VMEM((wide0 // 2, y1, nz), f32),
        pltpu.VMEM((wide1 // 2, take, LANES), f32),
        pltpu.VMEM((bx2 * by2, LANES), f32),
        pltpu.VMEM((nz // LANES, max(wide0, wide1, x2) // 2, max(y0, y1, rows2), LANES), f32),
        gather,
        gather,
        pltpu.SemaphoreType.DMA((2,)),
        [
            halo(3, THREE, bx, by, nz),
            halo(2, TWO, bx, by, nz),
            halo(2, TWO, bx, by, nz),
            halo(3, THREE, bx1, by1, LANES),
            halo(2, TWO, bx1, by1, LANES),
            halo(3, THREE, bx1, by1, LANES),
        ],
        pltpu.SemaphoreType.DMA((2 * (py_count - 1),)),
        pltpu.SemaphoreType.DMA((2 * (py_count - 1),)),
        pltpu.SemaphoreType.DMA((2 * (px_count - 1),)),
        pltpu.SemaphoreType.DMA((2 * (px_count - 1),)),
    ]
    return pl.pallas_call(
        functools.partial(kernel, (px_count, py_count)),
        out_shape=jax.ShapeDtypeStruct(source.shape, f32),
        in_specs=[pl.BlockSpec(memory_space=pl.ANY)] * 2,
        out_specs=pl.BlockSpec(memory_space=pltpu.VMEM),
        scratch_shapes=scratch,
        compiler_params=pltpu.CompilerParams(
            collective_id=0, has_side_effects=True, vmem_limit_bytes=56 * 1024 * 1024
        ),
    )(source, density)


def solution(mesh):
    spec = P("px", "py", None)
    return jax.shard_map(
        functools.partial(per_device, mesh.shape["px"], mesh.shape["py"]),
        mesh=mesh,
        in_specs=(spec, spec),
        out_specs=spec,
        check_vma=False,
    )
```

```python
import functools

import jax
import jax.numpy as jnp
from jax import lax
from jax.experimental import pallas as pl
from jax.experimental.pallas import tpu as pltpu
from jax.sharding import PartitionSpec as P

COARSE = 8
LANES = 128
HX0, HX1, HY, PAD2 = 4, 4, 4, 2
THREE, TWO = ((0, 2, 3), (2, 1, 3)), ((0, 2, 2),)
THREE0, TWO0 = ((0, 2, 2), (2, 1, 0)), ((0, 2, 1),)
ROWS = 8
DIRECTIONS = [(dx, dy) for dx in (-1, 0, 1) for dy in (-1, 0, 1) if (dx, dy) != (0, 0)]
MESH = pl.DeviceIdType.MESH


def iota(shape, dim):
    return lax.broadcasted_iota(jnp.int32, shape, dim)


def dot(a, b):
    return jnp.dot(a, b, precision=lax.Precision.HIGHEST, preferred_element_type=jnp.float32)


def matrix(shape, test, value):
    return jnp.where(test(iota(shape, 0), iota(shape, 1)), value, 0.0).astype(jnp.float32)


def loop(low, high, body, unroll=1):
    def step(i, carry):
        body(i)
        return carry

    lax.fori_loop(low, high, step, 0, unroll=unroll)


def chunks(low, high, size, most, body):
    count = high - low
    n = max(d for d in range(1, count + 1) if count % d == 0 and (d == 1 or d * size <= most))
    if n == count:
        body(low, n)
    else:
        loop(0, count // n, lambda i: body(low + i * n, n))


class Level:
    def __init__(self, refs, factor, start, total, rows, lanes, span, packed):
        (self.m, self.wx, self.wy, self.wz, self.k, self.g, self.u) = refs
        self.low, self.high = span
        self.half = 0.5 * factor
        self.start, self.total = start, total
        shape = self.m.shape[1:]
        self.shape, self.packed = shape, packed
        row, lane = iota(shape, 0), iota(shape, 1)
        first, total_y = rows
        nz, stride = lanes
        group = lane // stride if packed else 0
        gy = row + group * shape[0]
        if not packed:
            gy = first + jnp.where(row < shape[0] - HY, row, row - shape[0])
        gz = lane % stride if packed else lane
        self.row = row
        self.size = -(-shape[0] // ROWS) * (shape[1] // LANES)

        def keep(pos, count, span):
            plus = (pos != count - 1) & (pos != -1) & (pos != span - 1)
            minus = (pos != 0) & (pos != count)
            return jnp.where(plus, 1.0, 0.0), jnp.where(minus, 1.0, 0.0)

        self.kyp, self.kym = keep(gy, total_y, -9)
        self.kzp, self.kzm = keep(gz, nz, stride)
        self.gz, self.nz = gz, nz

    def y_minus(self, t):
        r = pltpu.roll(t, 1, t.ndim - 2)
        if self.packed:
            r = jnp.where(self.row == 0, pltpu.roll(r, LANES // 2, r.ndim - 1), r)
        return r

    def y_plus(self, t):
        r = pltpu.roll(t, self.shape[0] - 1, t.ndim - 2)
        if self.packed:
            r = jnp.where(self.row == self.shape[0] - 1, pltpu.roll(r, LANES // 2, r.ndim - 1), r)
        return r

    def z_minus(self, t):
        return pltpu.roll(t, 1, t.ndim - 1)

    def z_plus(self, t):
        return pltpu.roll(t, self.shape[1] - 1, t.ndim - 1)

    def clear(self, *refs):
        for i in (self.low - 1, self.high):
            for ref in refs:
                ref[i] = jnp.zeros(self.shape, jnp.float32)

    def face(self, x):
        gx = self.start + x
        return jnp.where((gx != self.total - 1) & (gx != -1), 1.0, 0.0)

    def setup(self, source=None):
        before = self.low - 1
        self.wx[before] = (self.half * self.face(before)) * (self.m[before] + self.m[self.low])
        known = self.kyp + self.kym + self.kzp + self.kzm

        def body(x, n):
            m = [self.m[x - 1 + j] for j in range(n + 2)]
            f = None if source is None else [source(x + j) for j in range(n)]
            k = [self.face(x - 1 + j) for j in range(n + 1)]
            s = [k[j] * (m[j] + m[j + 1]) for j in range(n + 1)]
            done = []
            for j in range(n):
                c = m[j + 1]
                wyp = self.kyp * (c + self.y_plus(c))
                wym = self.kym * (c + self.y_minus(c))
                wzp = self.kzp * (c + self.z_plus(c))
                wzm = self.kzm * (c + self.z_minus(c))
                missing = 6.0 - (k[j] + k[j + 1]) - known
                diag = ((s[j] + s[j + 1]) + (wyp + wym)) + ((wzp + wzm) + 2.0 * c * missing)
                done.append((self.half * s[j + 1], self.half * wyp, self.half * wzp,
                             0.8 / (self.half * diag)))
            for j, (wx, wy, wz, inverse) in enumerate(done):
                self.wx[x + j] = wx
                self.wy[x + j] = wy
                self.wz[x + j] = wz
                self.k[x + j] = inverse
                if f is not None:
                    self.g[x + j] = inverse * f[j]

        chunks(self.low, self.high, self.size, 12, body)

    def scale(self):
        def body(x, n):
            at = pl.ds(x, n)
            self.g[at] = self.k[at] * self.g[at]

        chunks(self.low, self.high, self.size, 24, body)

    def change(self, ref, x, n):
        at = pl.ds(x, n)
        v, wy, wz = ref[at], self.wy[at], self.wz[at]
        total = self.wx[at] * ref[pl.ds(x + 1, n)] + self.wx[pl.ds(x - 1, n)] * ref[pl.ds(x - 1, n)]
        total = total + (wy * self.y_plus(v) + self.y_minus(wy * v))
        total = total + (wz * self.z_plus(v) + self.z_minus(wz * v))
        return v, self.g[at] + self.k[at] * total

    def sweep(self, src, dst, inset=0):
        def body(x, n):
            v, rest = self.change(src, x, n)
            dst[pl.ds(x, n)] = 0.2 * v + rest

        chunks(self.low + inset, self.high - inset, self.size, 24, body)

    def residual(self, x, n):
        v, rest = self.change(self.u, x, n)
        return (rest - 0.8 * v) / self.k[pl.ds(x, n)]


def columns(width):
    return [slice(c, c + LANES) for c in range(0, width, LANES)]


def pair_slabs(tmp, i, value):
    count, rows, width = value.shape
    sums = [value[j] + value[j + 1] for j in range(0, count, 2)]
    for j, both in enumerate(sums):
        for k, c in enumerate(columns(width)):
            tmp[k, i + j, 0:rows] = both[:, c]


def pair_rows(tmp, count, rows, width):
    parts = [
        tmp[k, 0:count, pl.ds(0, rows, stride=2)] + tmp[k, 0:count, pl.ds(1, rows, stride=2)]
        for k in range(width // LANES)
    ]
    return parts[0] if len(parts) == 1 else jnp.concatenate(parts, 2)


def add_double(tmp, values, target, first, size):
    rows = 0
    for value in values:
        count, more, width = value.shape
        for k, c in enumerate(columns(width)):
            tmp[k, 0:count, pl.ds(2 * rows, more, stride=2)] = value[:, :, c]
            tmp[k, 0:count, pl.ds(2 * rows + 1, more, stride=2)] = value[:, :, c]
        rows += more

    def body(i, n):
        parts = [tmp[k, pl.ds(i, n), 0 : 2 * rows] for k in range(width // LANES)]
        e = parts[0] if len(parts) == 1 else jnp.concatenate(parts, 2)
        old = target[pl.ds(first + 2 * i, 2 * n)]
        new = [old[j] + e[j // 2] for j in range(2 * n)]
        for j in range(2 * n):
            target[first + 2 * i + j] = new[j]

    chunks(0, count, 2 * size, 24, body)


def kernel(sizes, source, density, out, den, src, l0, l1, l2, l3, pe0, pe1, t1, tmp,
           gm, gf, copy_sem, halos, sa, ra, sb, rb):
    px_count, py_count = sizes
    px, py = lax.axis_index("px"), lax.axis_index("py")
    bx, by, nz = source.shape
    nx, ny = bx * px_count, by * py_count
    bx1, by1, bx2, by2 = bx // 2, by // 2, bx // 4, by // 4

    def inside(dx, dy):
        test = None
        for d, pos, count in ((dx, px, px_count), (dy, py, py_count)):
            if d:
                one = (pos < count - 1) if d > 0 else (pos > 0)
                test = one if test is None else test & one
        return test

    class Halo:
        def __init__(self, refs, hx, pieces, block):
            self.xsend, self.xland, self.ysend, self.yland, self.send, self.recv = refs
            self.hx, self.pieces, self.block = hx, pieces, block

        def fill(self, value):
            edges = ((px == 0, 0, 0), (px == px_count - 1, 0, 1),
                     (py == 0, 1, 0), (py == py_count - 1, 1, 1))
            hx, bx = self.hx, self.block[0]
            for test, dim, side in edges:
                @pl.when(test)
                def _():
                    if dim == 0:
                        ref = self.xland
                        ref[side] = jnp.full(ref.shape[1:], value, jnp.float32)
                    for ref in self.yland:
                        if dim:
                            ref[side] = jnp.full(ref.shape[1:], value, jnp.float32)
                        else:
                            at = side * (hx + bx)
                            for s in range(2):
                                ref[s, at : at + hx] = jnp.full((hx,) + ref.shape[2:], value, jnp.float32)

        def pack(self, ref, ox):
            hx, (bx, by) = self.hx, self.block
            self.xsend[0] = ref[ox : ox + hx, 0:by]
            self.xsend[1] = ref[ox + bx - hx : ox + bx, 0:by]
            for ysend, (d, w, _) in zip(self.ysend, self.pieces):
                ysend[0] = ref[ox : ox + bx, d : d + w]
                ysend[1] = ref[ox : ox + bx, by - d - w : by - d]

        def each(self, act, sign):
            hx, bx = self.hx, self.block[0]
            n = 0
            for dx, dy in DIRECTIONS:
                if dy == 0:
                    side = (dx + 1) // 2
                    pairs = [(self.xsend.at[side], self.xland.at[1 - side])]
                else:
                    side = (dy + 1) // 2
                    pairs = []
                    for a, b, (_, _, corner) in zip(self.ysend, self.yland, self.pieces):
                        own, there, count = (
                            (0, hx + bx, corner), (0, hx, bx), (bx - corner, hx - corner, corner)
                        )[dx + 1]
                        if count:
                            pairs.append(
                                (a.at[side, pl.ds(own, count)], b.at[1 - side, pl.ds(there, count)])
                            )
                copies = []
                for a, b in pairs:
                    copies.append(pltpu.make_async_remote_copy(
                        src_ref=a,
                        dst_ref=b,
                        send_sem=self.send.at[n],
                        recv_sem=self.recv.at[n],
                        device_id=(px + dx, py + dy),
                        device_id_type=MESH,
                    ))
                    n += 1

                @pl.when(inside(sign * dx, sign * dy))
                def _():
                    for copy in copies:
                        act(copy)

        def start(self):
            self.each(lambda c: c.start(), 1)

        def arrive(self):
            self.each(lambda c: c.wait_recv(), -1)

        def sent(self):
            self.each(lambda c: c.wait_send(), 1)

        def unpack(self, ref, ox, change=lambda v: v):
            hx, (bx, by), rows = self.hx, self.block, ref.shape[1]
            ref[ox - hx : ox, 0:by] = change(self.xland[0])
            ref[ox + bx : ox + bx + hx, 0:by] = change(self.xland[1])
            for yland, (d, w, _) in zip(self.yland, self.pieces):
                ref[ox - hx : ox + bx + hx, rows - d - w : rows - d] = change(yland[0])
                ref[ox - hx : ox + bx + hx, by + d : by + d + w] = change(yland[1])

    def along(axis, ref, send, recv, base):
        count, me = (py_count, py) if axis else (px_count, px)
        region = ref.at[px, py] if axis else ref.at[px]

        def each(act):
            for k in range(1, count):
                to = lax.rem(me + k, count)
                act(pltpu.make_async_remote_copy(
                    src_ref=region,
                    dst_ref=region,
                    send_sem=send.at[base + k - 1],
                    recv_sem=recv.at[base + k - 1],
                    device_id=(px, to) if axis else (to, py),
                    device_id_type=MESH,
                ))

        def arrive(steps=range(1, count)):
            for k in steps:
                frm = lax.rem(me + count - k, count)
                landed = ref.at[px, frm] if axis else ref.at[frm]
                pltpu.make_async_remote_copy(
                    src_ref=landed,
                    dst_ref=landed,
                    send_sem=send.at[base + k - 1],
                    recv_sem=recv.at[base + k - 1],
                    device_id=(px, frm) if axis else (frm, py),
                    device_id_type=MESH,
                ).wait_recv()

        return (lambda: each(lambda c: c.start())), arrive, (lambda: each(lambda c: c.wait_send()))

    m0, f0, u0 = l0[0], l0[5], l0[6]
    m1, f1, u1 = l1[0], l1[5], l1[6]
    own_copies = [
        pltpu.make_async_copy(a, b, copy_sem.at[i])
        for i, (a, b) in enumerate(((density, den), (source, src)))
    ]
    for c in own_copies:
        c.start()
    block0, block1 = (bx, by), (bx1, by1)
    halo_m0 = Halo(halos[0], 3, THREE0, block0)
    halo_f0 = Halo(halos[1], 2, TWO0, block0)
    halo_u0 = Halo(halos[2], 2, TWO0, block0)
    halo_m1 = Halo(halos[3], 3, THREE, block1)
    halo_f1 = Halo(halos[4], 2, TWO, block1)
    halo_u1 = Halo(halos[5], 3, THREE, block1)
    all_halos = (halo_m0, halo_f0, halo_u0, halo_m1, halo_f1, halo_u1)
    for h, value in zip(all_halos, (1.0, 0.0, 0.0, 1.0, 0.0, 0.0)):
        h.fill(value)

    barrier = pltpu.get_barrier_semaphore()
    for k in range(1, py_count):
        pl.semaphore_signal(barrier, 1, device_id=(px, lax.rem(py + k, py_count)), device_id_type=MESH)
    for k in range(1, px_count):
        pl.semaphore_signal(barrier, 1, device_id=(lax.rem(px + k, px_count), py), device_id_type=MESH)
    for dx, dy in DIRECTIONS:
        if dx and dy:
            @pl.when(inside(dx, dy))
            def _():
                pl.semaphore_signal(barrier, 1, device_id=(px + dx, py + dy), device_id_type=MESH)
    beside_x = jnp.minimum(px, 1) + jnp.minimum(px_count - 1 - px, 1)
    beside_y = jnp.minimum(py, 1) + jnp.minimum(py_count - 1 - py, 1)
    own_copies[0].wait()
    halo_m0.pack(den, 0)
    pl.semaphore_wait(barrier, px_count + py_count - 2 + beside_x * beside_y)

    halo_m0.start()
    own_copies[1].wait()
    halo_f0.pack(src, 0)
    halo_f0.start()

    r_fine = matrix((nz, LANES), lambda z, c: z // 2 == c, 0.125)
    r_low = matrix((LANES, LANES), lambda z, c: z // 2 == c, 0.125)
    r_high = matrix((LANES, LANES), lambda z, c: z // 2 + LANES // 2 == c, 0.125)
    half = LANES // 2
    r_pack = matrix(
        (LANES, LANES), lambda z, c: (z // half == c // half) & ((z % half) // 2 == c % half), 0.125
    )

    def restrict0(get, dst):
        def body(i, n):
            pair_slabs(tmp, i, get(HX0 + 2 * i, 2 * n))

        chunks(0, bx1, 2 * (y0 // ROWS) * (nz // LANES), 24, body)
        value = dot(pair_rows(tmp, bx1, by1, nz).reshape(bx1 * by1, nz), r_fine)
        dst[HX1 : HX1 + bx1, 0:by1] = value.reshape(bx1, by1, LANES)

    def restrict1(get, dst):
        def body(i, n):
            pair_slabs(tmp, i, get(HX1 + 2 * i, 2 * n))

        chunks(0, bx2, 2 * (y1 // ROWS), 24, body)
        sums = pair_rows(tmp, bx2, by2, LANES)
        for i in range(bx2):
            t1[i * by2 : (i + 1) * by2] = sums[i]
        n = bx2 * by2 // 2
        dst[px, py] = dot(t1[0:n], r_low) + dot(t1[n : 2 * n], r_high)

    wide0, wide1, wide2, wide3 = (l[0].shape[0] for l in (l0, l1, l2, l3))
    y0, y1 = l0[0].shape[1], l1[0].shape[1]

    def own(x, n):
        m0[pl.ds(HX0 + x, n), 0:by] = 1.0 / den[pl.ds(x, n)]
        f0[pl.ds(HX0 + x, n), 0:by] = src[pl.ds(x, n)]

    chunks(0, bx, (by // ROWS) * (nz // LANES), 24, own)
    restrict0(lambda x, n: m0[pl.ds(x, n), 0:by], m1)
    halo_m1.pack(m1, HX1)
    halo_m1.start()
    restrict1(lambda x, n: m1[pl.ds(x, n), 0:by1], gm)
    ma_start, ma_arrive, ma_sent = along(1, gm, sa, ra, 0)
    fa_start, fa_arrive, fa_sent = along(1, gf, sa, ra, py_count - 1)
    mb_start, mb_arrive, mb_sent = along(0, gm, sb, rb, 0)
    _, fb_arrive, fb_sent = along(0, gf, sb, rb, px_count - 1)
    ma_start()

    def forward(k):
        block = gf.at[px, lax.rem(py + py_count - k, py_count)]
        for step in range(1, px_count):
            pltpu.make_async_remote_copy(
                src_ref=block,
                dst_ref=block,
                send_sem=sb.at[px_count - 1 + step - 1],
                recv_sem=rb.at[px_count - 1 + step - 1],
                device_id=(lax.rem(px + step, px_count), py),
                device_id_type=MESH,
            ).start()

    level0 = Level(l0, 1.0, px * bx - HX0, nx, (py * by, ny), (nz, nz), (HX0 - 2, HX0 + bx + 2), False)
    level1 = Level(l1, 0.25, px * bx1 - HX1, nx // 2, (py * by1, ny // 2),
                   (nz // 2, LANES), (HX1 - 2, HX1 + bx1 + 2), False)
    level2 = Level(l2, 0.25**2, -PAD2, nx // 4, (0, ny // 4), (nz // 4, half),
                   (PAD2, wide2 - PAD2), True)
    level3 = Level(l3, 0.25**3, -1, nx // 8, (0, ny // 8), (nz // 8, half), (1, wide3 - 1), True)
    level2.clear(level2.g, level2.u)
    level3.clear(level3.g, level3.u)

    def spread(gathered, dst):
        n = bx2 // 2
        lane = iota((n * by2, LANES), 1)
        groups = py_count // 2

        def body(p):
            for q in range(groups):
                a, b = gathered[p, q], gathered[p, q + groups]
                first = jnp.where(lane < half, a, pltpu.roll(b, half, 1))
                second = jnp.where(lane < half, pltpu.roll(a, half, 1), b)
                for i in range(n):
                    rows = slice(q * by2, (q + 1) * by2)
                    piece = slice(i * by2, (i + 1) * by2)
                    dst[PAD2 + p * bx2 + i, rows] = first[piece]
                    dst[PAD2 + p * bx2 + n + i, rows] = second[piece]

        loop(0, px_count, body)

    def pair2(get, dst):
        count = wide3 - 2
        rows = l3[0].shape[1]

        def body(i, n):
            pair_slabs(tmp, i, get(PAD2 + 2 * i, 2 * n))

        chunks(0, count, 2 * level2.size, 24, body)
        sums = pair_rows(tmp, count, rows, LANES)
        dst[1 : 1 + count] = dot(sums.reshape(count * rows, LANES), r_pack).reshape(
            count, rows, LANES
        )

    halo_m0.arrive()
    halo_m0.unpack(m0, HX0, lambda v: 1.0 / v)
    level0.setup()
    halo_f0.arrive()
    halo_f0.unpack(f0, HX0)
    ma_arrive()
    mb_start()
    level0.scale()
    level0.sweep(f0, u0, 1)
    restrict0(lambda x, n: level0.residual(x, n)[:, 0:by], f1)
    halo_f1.pack(f1, HX1)
    halo_f1.start()
    halo_u0.pack(u0, HX0)

    halo_m1.arrive()
    halo_m1.unpack(m1, HX1)
    level1.setup()
    mb_arrive()
    one2 = jnp.ones((PAD2,) + level2.shape, jnp.float32)
    one3 = jnp.ones(level3.shape, jnp.float32)
    m2, m3 = l2[0], l3[0]
    spread(gm, m2)
    m2[0:PAD2] = one2
    m2[wide2 - PAD2 :] = one2
    level2.setup()
    halo_f1.arrive()
    halo_f1.unpack(f1, HX1)
    level1.scale()
    level1.sweep(f1, u1, 1)
    restrict1(lambda x, n: level1.residual(x, n)[:, 0:by1], gf)
    fa_start()
    forward(0)
    halo_u1.pack(u1, HX1)
    pair2(lambda x, n: m2[pl.ds(x, n)], m3)
    m3[0] = one3
    m3[wide3 - 1] = one3

    inner3 = slice(1, wide3 - 1)
    m3[inner3] = jnp.where(level3.gz < level3.nz, m3[inner3], 1.0)
    level3.setup()


    for k in sorted(range(1, py_count), key=lambda k: (min(k, py_count - k), k)):
        fa_arrive([k])
        forward(k)
    halo_u1.start()
    halo_u0.start()
    fb_arrive()
    f2, f3 = l2[5], l3[5]
    spread(gf, f2)

    level2.scale()
    level2.sweep(level2.g, level2.u)
    pair2(level2.residual, f3)

    level3.scale()
    m3[0] = jnp.zeros(level3.shape, jnp.float32)
    m3[wide3 - 1] = jnp.zeros(level3.shape, jnp.float32)
    level3.sweep(f3, level3.u)
    now, later = level3.u, m3
    for _ in range(COARSE - 2):
        level3.sweep(now, later)
        now, later = later, now

    p_pack = matrix(
        (LANES, LANES), lambda k, z: (z // half == k // half) & ((z % half) // 2 == k % half), 1.0
    )
    count3, rows3 = wide3 - 2, l3[0].shape[1]
    e3 = dot(now[1 : 1 + count3].reshape(count3 * rows3, LANES), p_pack)
    add_double(tmp, [e3.reshape(count3, rows3, LANES)], level2.u, PAD2, level2.size)
    zero2 = jnp.zeros((PAD2,) + level2.shape, jnp.float32)
    m2[0:PAD2] = zero2
    m2[wide2 - PAD2 :] = zero2
    level2.u[0:PAD2] = zero2
    level2.u[wide2 - PAD2 :] = zero2
    level2.sweep(level2.u, m2)
    level2.sweep(m2, level2.u)

    full = 2 * level2.shape[0]
    shift = lax.rem(full - py * by2, full)
    near = by2 + HY // 2

    halo_u1.arrive()
    halo_u1.unpack(u1, HX1)

    def fetch(c, n):
        e = [level2.u[px * bx2 + c + j] for j in range(n)]
        e = [jnp.concatenate([one, pltpu.roll(one, half, 1)], 0) for one in e]
        e = [pltpu.roll(one, shift, 0) for one in e]
        for j in range(n):
            pe1[c + j, 0:near] = e[j][0:near]
            pe1[c + j, near : near + HY // 2] = e[j][full - HY // 2 : full]

    chunks(0, wide1 // 2, 2 * level2.size, 32, fetch)
    p_one = matrix((LANES, LANES), lambda k, z: z // 2 == k, 1.0)
    e2 = dot(pe1[...].reshape(-1, LANES), p_one).reshape(pe1.shape)
    add_double(tmp, [e2[:, 0 : y1 // 2]], level1.u, 0, level1.size)
    level1.sweep(u1, m1)
    level1.sweep(m1, u1, 1)

    p_zero = matrix((LANES, nz), lambda k, z: z // 2 == k, 1.0)
    base = HX1 - HX0 // 2
    count = wide0 // 2
    e1 = dot(level1.u[base : base + count].reshape(count * y1, LANES), p_zero)
    pe0[...] = e1.reshape(pe0.shape)
    halo_u0.arrive()
    halo_u0.unpack(u0, HX0)
    parts = [pe0[:, 0 : by1 + HY // 2], pe0[:, y1 - HY // 2 : y1]]
    add_double(tmp, parts, level0.u, 0, level0.size)
    level0.sweep(u0, m0, 1)

    def last(x, n):
        v, rest = level0.change(m0, HX0 + x, n)
        out[pl.ds(x, n)] = (0.2 * v + rest)[:, 0:by]

    chunks(0, bx, level0.size, 24, last)

    for h in all_halos:
        h.sent()
    for done in (ma_sent, mb_sent, fa_sent, fb_sent):
        done()


def per_device(px_count, py_count, source, density):
    bx, by, nz = source.shape
    f32 = jnp.float32
    bx1, by1, bx2, by2 = bx // 2, by // 2, bx // 4, by // 4

    def level(wide, rows, lanes):
        return [pltpu.VMEM((wide, rows, lanes), f32)] * 7

    y0, y1 = by + 2 * HY, by1 + 2 * HY
    wide0, wide1 = bx + 2 * HX0, bx1 + 2 * HX1
    x2, rows2 = bx2 * px_count, by2 * py_count // 2
    ext = pltpu.VMEM(source.shape, f32)

    def halo(hx, pieces, rows, cols, lanes):
        copies = pltpu.SemaphoreType.DMA((2 + sum(6 if c else 2 for _, _, c in pieces),))
        return [
            pltpu.VMEM((2, hx, cols, lanes), f32),
            pltpu.VMEM((2, hx, cols, lanes), f32),
            [pltpu.VMEM((2, rows, w, lanes), f32) for _, w, _ in pieces],
            [pltpu.VMEM((2, rows + 2 * hx, w, lanes), f32) for _, w, _ in pieces],
            copies,
            copies,
        ]

    take = -(-(y1 // 2) // ROWS) * ROWS
    gather = pltpu.VMEM((px_count, py_count, bx2 * by2 // 2, LANES), f32)
    scratch = [
        ext,
        ext,
        level(wide0, y0, nz),
        level(wide1, y1, LANES),
        level(x2 + 2 * PAD2, rows2, LANES),
        level(x2 // 2 + 2, rows2 // 2, LANES),
        pltpu.VMEM((wide0 // 2, y1, nz), f32),
        pltpu.VMEM((wide1 // 2, take, LANES), f32),
        pltpu.VMEM((bx2 * by2, LANES), f32),
        pltpu.VMEM((nz // LANES, max(wide0, wide1, x2) // 2, max(y0, y1, rows2), LANES), f32),
        gather,
        gather,
        pltpu.SemaphoreType.DMA((2,)),
        [
            halo(3, THREE0, bx, by, nz),
            halo(2, TWO0, bx, by, nz),
            halo(2, TWO0, bx, by, nz),
            halo(3, THREE, bx1, by1, LANES),
            halo(2, TWO, bx1, by1, LANES),
            halo(3, THREE, bx1, by1, LANES),
        ],
        pltpu.SemaphoreType.DMA((2 * (py_count - 1),)),
        pltpu.SemaphoreType.DMA((2 * (py_count - 1),)),
        pltpu.SemaphoreType.DMA((2 * (px_count - 1),)),
        pltpu.SemaphoreType.DMA((2 * (px_count - 1),)),
    ]
    return pl.pallas_call(
        functools.partial(kernel, (px_count, py_count)),
        out_shape=jax.ShapeDtypeStruct(source.shape, f32),
        in_specs=[pl.BlockSpec(memory_space=pl.ANY)] * 2,
        out_specs=pl.BlockSpec(memory_space=pltpu.VMEM),
        scratch_shapes=scratch,
        compiler_params=pltpu.CompilerParams(
            collective_id=0, has_side_effects=True, vmem_limit_bytes=56 * 1024 * 1024
        ),
    )(source, density)


def solution(mesh):
    spec = P("px", "py", None)
    return jax.shard_map(
        functools.partial(per_device, mesh.shape["px"], mesh.shape["py"]),
        mesh=mesh,
        in_specs=(spec, spec),
        out_specs=spec,
        check_vma=False,
    )
```

```python
import functools

import jax
import jax.numpy as jnp
from jax import lax
from jax.experimental import pallas as pl
from jax.experimental.pallas import tpu as pltpu
from jax.sharding import PartitionSpec as P

COARSE = 8
OUT_PARTS = 4
LANES = 128
HX0, HX1, HY, PAD2 = 4, 4, 4, 2
THREE, TWO = ((0, 2, 3), (2, 1, 3)), ((0, 2, 2),)
THREE0, TWO0 = ((0, 2, 2), (2, 1, 0)), ((0, 2, 1),)
ROWS = 8
DIRECTIONS = [(dx, dy) for dx in (-1, 0, 1) for dy in (-1, 0, 1) if (dx, dy) != (0, 0)]
MESH = pl.DeviceIdType.MESH


def iota(shape, dim):
    return lax.broadcasted_iota(jnp.int32, shape, dim)


def dot(a, b):
    total = None
    for _ in range(3):
        part = a.astype(jnp.bfloat16)
        a = a - part.astype(jnp.float32)
        term = jnp.dot(part, b, preferred_element_type=jnp.float32)
        total = term if total is None else total + term
    return total


def matrix(shape, test, value):
    chosen = jnp.where(test(iota(shape, 0), iota(shape, 1)), value, 0.0)
    return chosen.astype(jnp.bfloat16)


def loop(low, high, body, unroll=1):
    def step(i, carry):
        body(i)
        return carry

    lax.fori_loop(low, high, step, 0, unroll=unroll)


def chunks(low, high, size, most, body):
    count = high - low
    n = max(d for d in range(1, count + 1) if count % d == 0 and (d == 1 or d * size <= most))
    if n == count:
        body(low, n)
    else:
        loop(0, count // n, lambda i: body(low + i * n, n))


class Level:
    def __init__(self, refs, factor, start, total, rows, lanes, span, packed):
        (self.m, self.wx, self.wy, self.wz, self.k, self.g, self.u) = refs
        self.low, self.high = span
        self.half = 0.5 * factor
        self.start, self.total = start, total
        shape = self.m.shape[1:]
        self.shape, self.packed = shape, packed
        row, lane = iota(shape, 0), iota(shape, 1)
        first, total_y = rows
        nz, stride = lanes
        group = lane // stride if packed else 0
        gy = row + group * shape[0]
        if not packed:
            gy = first + jnp.where(row < shape[0] - HY, row, row - shape[0])
        gz = lane % stride if packed else lane
        self.row = row
        self.size = -(-shape[0] // ROWS) * (shape[1] // LANES)

        def keep(pos, count, span):
            plus = (pos != count - 1) & (pos != -1) & (pos != span - 1)
            minus = (pos != 0) & (pos != count)
            return jnp.where(plus, 1.0, 0.0), jnp.where(minus, 1.0, 0.0)

        self.kyp, self.kym = keep(gy, total_y, -9)
        self.kzp, self.kzm = keep(gz, nz, stride)
        self.gz, self.nz = gz, nz

    def y_minus(self, t):
        r = pltpu.roll(t, 1, t.ndim - 2)
        if self.packed:
            r = jnp.where(self.row == 0, pltpu.roll(r, LANES // 2, r.ndim - 1), r)
        return r

    def y_plus(self, t):
        r = pltpu.roll(t, self.shape[0] - 1, t.ndim - 2)
        if self.packed:
            r = jnp.where(self.row == self.shape[0] - 1, pltpu.roll(r, LANES // 2, r.ndim - 1), r)
        return r

    def z_minus(self, t):
        return pltpu.roll(t, 1, t.ndim - 1)

    def z_plus(self, t):
        return pltpu.roll(t, self.shape[1] - 1, t.ndim - 1)

    def clear(self, *refs):
        for i in (self.low - 1, self.high):
            for ref in refs:
                ref[i] = jnp.zeros(self.shape, jnp.float32)

    def face(self, x):
        gx = self.start + x
        return jnp.where((gx != self.total - 1) & (gx != -1), 1.0, 0.0)

    def setup(self, source=None):
        before = self.low - 1
        self.wx[before] = (self.half * self.face(before)) * (self.m[before] + self.m[self.low])
        known = self.kyp + self.kym + self.kzp + self.kzm

        def body(x, n):
            m = [self.m[x - 1 + j] for j in range(n + 2)]
            f = None if source is None else [source(x + j) for j in range(n)]
            k = [self.face(x - 1 + j) for j in range(n + 1)]
            s = [k[j] * (m[j] + m[j + 1]) for j in range(n + 1)]
            done = []
            for j in range(n):
                c = m[j + 1]
                wyp = self.kyp * (c + self.y_plus(c))
                wym = self.kym * (c + self.y_minus(c))
                wzp = self.kzp * (c + self.z_plus(c))
                wzm = self.kzm * (c + self.z_minus(c))
                missing = 6.0 - (k[j] + k[j + 1]) - known
                diag = ((s[j] + s[j + 1]) + (wyp + wym)) + ((wzp + wzm) + 2.0 * c * missing)
                done.append((self.half * s[j + 1], self.half * wyp, self.half * wzp,
                             0.8 / (self.half * diag)))
            for j, (wx, wy, wz, inverse) in enumerate(done):
                self.wx[x + j] = wx
                self.wy[x + j] = wy
                self.wz[x + j] = wz
                self.k[x + j] = inverse
                if f is not None:
                    self.g[x + j] = inverse * f[j]

        chunks(self.low, self.high, self.size, 12, body)

    def scale(self):
        def body(x, n):
            at = pl.ds(x, n)
            self.g[at] = self.k[at] * self.g[at]

        chunks(self.low, self.high, self.size, 24, body)

    def change(self, ref, x, n):
        at = pl.ds(x, n)
        v, wy, wz = ref[at], self.wy[at], self.wz[at]
        total = self.wx[at] * ref[pl.ds(x + 1, n)] + self.wx[pl.ds(x - 1, n)] * ref[pl.ds(x - 1, n)]
        total = total + (wy * self.y_plus(v) + self.y_minus(wy * v))
        total = total + (wz * self.z_plus(v) + self.z_minus(wz * v))
        return v, self.g[at] + self.k[at] * total

    def sweep(self, src, dst, inset=0):
        def body(x, n):
            v, rest = self.change(src, x, n)
            dst[pl.ds(x, n)] = 0.2 * v + rest

        chunks(self.low + inset, self.high - inset, self.size, 24, body)

    def residual(self, x, n):
        v, rest = self.change(self.u, x, n)
        return (rest - 0.8 * v) / self.k[pl.ds(x, n)]


def columns(width):
    return [slice(c, c + LANES) for c in range(0, width, LANES)]


def pair_slabs(tmp, i, value):
    count, rows, width = value.shape
    sums = [value[j] + value[j + 1] for j in range(0, count, 2)]
    for j, both in enumerate(sums):
        for k, c in enumerate(columns(width)):
            tmp[k, i + j, 0:rows] = both[:, c]


def pair_rows(tmp, count, rows, width):
    parts = [
        tmp[k, 0:count, pl.ds(0, rows, stride=2)] + tmp[k, 0:count, pl.ds(1, rows, stride=2)]
        for k in range(width // LANES)
    ]
    return parts[0] if len(parts) == 1 else jnp.concatenate(parts, 2)


def add_double(tmp, values, target, first, size):
    rows = 0
    for value in values:
        count, more, width = value.shape
        for k, c in enumerate(columns(width)):
            tmp[k, 0:count, pl.ds(2 * rows, more, stride=2)] = value[:, :, c]
            tmp[k, 0:count, pl.ds(2 * rows + 1, more, stride=2)] = value[:, :, c]
        rows += more

    def body(i, n):
        parts = [tmp[k, pl.ds(i, n), 0 : 2 * rows] for k in range(width // LANES)]
        e = parts[0] if len(parts) == 1 else jnp.concatenate(parts, 2)
        old = target[pl.ds(first + 2 * i, 2 * n)]
        new = [old[j] + e[j // 2] for j in range(2 * n)]
        for j in range(2 * n):
            target[first + 2 * i + j] = new[j]

    chunks(0, count, 2 * size, 24, body)


def kernel(sizes, source, density, out, den, src, l0, l1, l2, l3, pe0, pe1, t1, tmp,
           gm, gf, copy_sem, halos, sa, ra, sb, rb):
    px_count, py_count = sizes
    px, py = lax.axis_index("px"), lax.axis_index("py")
    bx, by, nz = source.shape
    nx, ny = bx * px_count, by * py_count
    bx1, by1, bx2, by2 = bx // 2, by // 2, bx // 4, by // 4

    def inside(dx, dy):
        test = None
        for d, pos, count in ((dx, px, px_count), (dy, py, py_count)):
            if d:
                one = (pos < count - 1) if d > 0 else (pos > 0)
                test = one if test is None else test & one
        return test

    class Halo:
        def __init__(self, refs, hx, pieces, block):
            self.xsend, self.xland, self.ysend, self.yland, self.send, self.recv = refs
            self.hx, self.pieces, self.block = hx, pieces, block

        def fill(self, value):
            edges = ((px == 0, 0, 0), (px == px_count - 1, 0, 1),
                     (py == 0, 1, 0), (py == py_count - 1, 1, 1))
            hx, bx = self.hx, self.block[0]
            for test, dim, side in edges:
                @pl.when(test)
                def _():
                    if dim == 0:
                        ref = self.xland
                        ref[side] = jnp.full(ref.shape[1:], value, jnp.float32)
                    for ref in self.yland:
                        if dim:
                            ref[side] = jnp.full(ref.shape[1:], value, jnp.float32)
                        else:
                            at = side * (hx + bx)
                            for s in range(2):
                                ref[s, at : at + hx] = jnp.full((hx,) + ref.shape[2:], value, jnp.float32)

        def pack(self, ref, ox):
            hx, (bx, by) = self.hx, self.block
            self.xsend[0] = ref[ox : ox + hx, 0:by]
            self.xsend[1] = ref[ox + bx - hx : ox + bx, 0:by]
            for ysend, (d, w, _) in zip(self.ysend, self.pieces):
                ysend[0] = ref[ox : ox + bx, d : d + w]
                ysend[1] = ref[ox : ox + bx, by - d - w : by - d]

        def each(self, act, sign):
            hx, bx = self.hx, self.block[0]
            n = 0
            for dx, dy in DIRECTIONS:
                if dy == 0:
                    side = (dx + 1) // 2
                    pairs = [(self.xsend.at[side], self.xland.at[1 - side])]
                else:
                    side = (dy + 1) // 2
                    pairs = []
                    for a, b, (_, _, corner) in zip(self.ysend, self.yland, self.pieces):
                        own, there, count = (
                            (0, hx + bx, corner), (0, hx, bx), (bx - corner, hx - corner, corner)
                        )[dx + 1]
                        if count:
                            pairs.append(
                                (a.at[side, pl.ds(own, count)], b.at[1 - side, pl.ds(there, count)])
                            )
                copies = []
                for a, b in pairs:
                    copies.append(pltpu.make_async_remote_copy(
                        src_ref=a,
                        dst_ref=b,
                        send_sem=self.send.at[n],
                        recv_sem=self.recv.at[n],
                        device_id=(px + dx, py + dy),
                        device_id_type=MESH,
                    ))
                    n += 1

                @pl.when(inside(sign * dx, sign * dy))
                def _():
                    for copy in copies:
                        act(copy)

        def start(self):
            self.each(lambda c: c.start(), 1)

        def arrive(self):
            self.each(lambda c: c.wait_recv(), -1)

        def sent(self):
            self.each(lambda c: c.wait_send(), 1)

        def unpack(self, ref, ox, change=lambda v: v):
            hx, (bx, by), rows = self.hx, self.block, ref.shape[1]
            ref[ox - hx : ox, 0:by] = change(self.xland[0])
            ref[ox + bx : ox + bx + hx, 0:by] = change(self.xland[1])
            for yland, (d, w, _) in zip(self.yland, self.pieces):
                ref[ox - hx : ox + bx + hx, rows - d - w : rows - d] = change(yland[0])
                ref[ox - hx : ox + bx + hx, by + d : by + d + w] = change(yland[1])

    def along(axis, ref, send, recv, base):
        count, me = (py_count, py) if axis else (px_count, px)
        region = ref.at[px, py] if axis else ref.at[px]

        def each(act):
            for k in range(1, count):
                to = lax.rem(me + k, count)
                act(pltpu.make_async_remote_copy(
                    src_ref=region,
                    dst_ref=region,
                    send_sem=send.at[base + k - 1],
                    recv_sem=recv.at[base + k - 1],
                    device_id=(px, to) if axis else (to, py),
                    device_id_type=MESH,
                ))

        def arrive(steps=range(1, count)):
            for k in steps:
                frm = lax.rem(me + count - k, count)
                landed = ref.at[px, frm] if axis else ref.at[frm]
                pltpu.make_async_remote_copy(
                    src_ref=landed,
                    dst_ref=landed,
                    send_sem=send.at[base + k - 1],
                    recv_sem=recv.at[base + k - 1],
                    device_id=(px, frm) if axis else (frm, py),
                    device_id_type=MESH,
                ).wait_recv()

        return (lambda: each(lambda c: c.start())), arrive, (lambda: each(lambda c: c.wait_send()))

    m0, f0, u0 = l0[0], l0[5], l0[6]
    m1, f1, u1 = l1[0], l1[5], l1[6]
    own_copies = [
        pltpu.make_async_copy(a, b, copy_sem.at[i])
        for i, (a, b) in enumerate(((density, den), (source, src)))
    ]
    for c in own_copies:
        c.start()
    block0, block1 = (bx, by), (bx1, by1)
    halo_m0 = Halo(halos[0], 3, THREE0, block0)
    halo_f0 = Halo(halos[1], 2, TWO0, block0)
    halo_u0 = Halo(halos[2], 2, TWO0, block0)
    halo_m1 = Halo(halos[3], 3, THREE, block1)
    halo_f1 = Halo(halos[4], 2, TWO, block1)
    halo_u1 = Halo(halos[5], 3, THREE, block1)
    all_halos = (halo_m0, halo_f0, halo_u0, halo_m1, halo_f1, halo_u1)
    for h, value in zip(all_halos, (1.0, 0.0, 0.0, 1.0, 0.0, 0.0)):
        h.fill(value)

    barrier = pltpu.get_barrier_semaphore()
    for k in range(1, py_count):
        pl.semaphore_signal(barrier, 1, device_id=(px, lax.rem(py + k, py_count)), device_id_type=MESH)
    for k in range(1, px_count):
        pl.semaphore_signal(barrier, 1, device_id=(lax.rem(px + k, px_count), py), device_id_type=MESH)
    for dx, dy in DIRECTIONS:
        if dx and dy:
            @pl.when(inside(dx, dy))
            def _():
                pl.semaphore_signal(barrier, 1, device_id=(px + dx, py + dy), device_id_type=MESH)
    beside_x = jnp.minimum(px, 1) + jnp.minimum(px_count - 1 - px, 1)
    beside_y = jnp.minimum(py, 1) + jnp.minimum(py_count - 1 - py, 1)
    own_copies[0].wait()
    halo_m0.pack(den, 0)
    pl.semaphore_wait(barrier, px_count + py_count - 2 + beside_x * beside_y)

    halo_m0.start()
    own_copies[1].wait()
    halo_f0.pack(src, 0)
    halo_f0.start()

    r_fine = matrix((nz, LANES), lambda z, c: z // 2 == c, 0.125)
    r_low = matrix((LANES, LANES), lambda z, c: z // 2 == c, 0.125)
    r_high = matrix((LANES, LANES), lambda z, c: z // 2 + LANES // 2 == c, 0.125)
    half = LANES // 2
    r_pack = matrix(
        (LANES, LANES), lambda z, c: (z // half == c // half) & ((z % half) // 2 == c % half), 0.125
    )

    def restrict0(get, dst):
        def body(i, n):
            pair_slabs(tmp, i, get(HX0 + 2 * i, 2 * n))

        chunks(0, bx1, 2 * (y0 // ROWS) * (nz // LANES), 24, body)
        value = dot(pair_rows(tmp, bx1, by1, nz).reshape(bx1 * by1, nz), r_fine)
        dst[HX1 : HX1 + bx1, 0:by1] = value.reshape(bx1, by1, LANES)

    def restrict1(get, dst):
        def body(i, n):
            pair_slabs(tmp, i, get(HX1 + 2 * i, 2 * n))

        chunks(0, bx2, 2 * (y1 // ROWS), 24, body)
        sums = pair_rows(tmp, bx2, by2, LANES)
        for i in range(bx2):
            t1[i * by2 : (i + 1) * by2] = sums[i]
        n = bx2 * by2 // 2
        dst[px, py] = dot(t1[0:n], r_low) + dot(t1[n : 2 * n], r_high)

    wide0, wide1, wide2, wide3 = (l[0].shape[0] for l in (l0, l1, l2, l3))
    y0, y1 = l0[0].shape[1], l1[0].shape[1]

    def own(x, n):
        m0[pl.ds(HX0 + x, n), 0:by] = 1.0 / den[pl.ds(x, n)]
        f0[pl.ds(HX0 + x, n), 0:by] = src[pl.ds(x, n)]

    chunks(0, bx, (by // ROWS) * (nz // LANES), 24, own)
    restrict0(lambda x, n: m0[pl.ds(x, n), 0:by], m1)
    halo_m1.pack(m1, HX1)
    halo_m1.start()
    restrict1(lambda x, n: m1[pl.ds(x, n), 0:by1], gm)
    ma_start, ma_arrive, ma_sent = along(1, gm, sa, ra, 0)
    fa_start, fa_arrive, fa_sent = along(1, gf, sa, ra, py_count - 1)
    mb_start, mb_arrive, mb_sent = along(0, gm, sb, rb, 0)
    _, fb_arrive, fb_sent = along(0, gf, sb, rb, px_count - 1)
    ma_start()

    def forward(k):
        block = gf.at[px, lax.rem(py + py_count - k, py_count)]
        for step in range(1, px_count):
            pltpu.make_async_remote_copy(
                src_ref=block,
                dst_ref=block,
                send_sem=sb.at[px_count - 1 + step - 1],
                recv_sem=rb.at[px_count - 1 + step - 1],
                device_id=(lax.rem(px + step, px_count), py),
                device_id_type=MESH,
            ).start()

    level0 = Level(l0, 1.0, px * bx - HX0, nx, (py * by, ny), (nz, nz), (HX0 - 2, HX0 + bx + 2), False)
    level1 = Level(l1, 0.25, px * bx1 - HX1, nx // 2, (py * by1, ny // 2),
                   (nz // 2, LANES), (HX1 - 2, HX1 + bx1 + 2), False)
    level2 = Level(l2, 0.25**2, -PAD2, nx // 4, (0, ny // 4), (nz // 4, half),
                   (PAD2, wide2 - PAD2), True)
    level3 = Level(l3, 0.25**3, -1, nx // 8, (0, ny // 8), (nz // 8, half), (1, wide3 - 1), True)
    level2.clear(level2.g, level2.u)
    level3.clear(level3.g, level3.u)

    def spread(gathered, dst):
        n = bx2 // 2
        lane = iota((n * by2, LANES), 1)
        groups = py_count // 2

        def body(p):
            for q in range(groups):
                a, b = gathered[p, q], gathered[p, q + groups]
                first = jnp.where(lane < half, a, pltpu.roll(b, half, 1))
                second = jnp.where(lane < half, pltpu.roll(a, half, 1), b)
                for i in range(n):
                    rows = slice(q * by2, (q + 1) * by2)
                    piece = slice(i * by2, (i + 1) * by2)
                    dst[PAD2 + p * bx2 + i, rows] = first[piece]
                    dst[PAD2 + p * bx2 + n + i, rows] = second[piece]

        loop(0, px_count, body)

    def pair2(get, dst):
        count = wide3 - 2
        rows = l3[0].shape[1]

        def body(i, n):
            pair_slabs(tmp, i, get(PAD2 + 2 * i, 2 * n))

        chunks(0, count, 2 * level2.size, 24, body)
        sums = pair_rows(tmp, count, rows, LANES)
        dst[1 : 1 + count] = dot(sums.reshape(count * rows, LANES), r_pack).reshape(
            count, rows, LANES
        )

    halo_m0.arrive()
    halo_m0.unpack(m0, HX0, lambda v: 1.0 / v)
    level0.setup()
    halo_f0.arrive()
    halo_f0.unpack(f0, HX0)
    ma_arrive()
    mb_start()
    level0.scale()
    level0.sweep(f0, u0, 1)
    restrict0(lambda x, n: level0.residual(x, n)[:, 0:by], f1)
    halo_f1.pack(f1, HX1)
    halo_f1.start()
    halo_u0.pack(u0, HX0)

    halo_m1.arrive()
    halo_m1.unpack(m1, HX1)
    level1.setup()
    mb_arrive()
    one2 = jnp.ones((PAD2,) + level2.shape, jnp.float32)
    one3 = jnp.ones(level3.shape, jnp.float32)
    m2, m3 = l2[0], l3[0]
    spread(gm, m2)
    m2[0:PAD2] = one2
    m2[wide2 - PAD2 :] = one2
    level2.setup()
    halo_f1.arrive()
    halo_f1.unpack(f1, HX1)
    level1.scale()
    level1.sweep(f1, u1, 1)
    restrict1(lambda x, n: level1.residual(x, n)[:, 0:by1], gf)
    fa_start()
    forward(0)
    halo_u1.pack(u1, HX1)
    pair2(lambda x, n: m2[pl.ds(x, n)], m3)
    m3[0] = one3
    m3[wide3 - 1] = one3

    inner3 = slice(1, wide3 - 1)
    m3[inner3] = jnp.where(level3.gz < level3.nz, m3[inner3], 1.0)
    level3.setup()


    for k in sorted(range(1, py_count), key=lambda k: (min(k, py_count - k), k)):
        fa_arrive([k])
        forward(k)
    halo_u1.start()
    halo_u0.start()
    fb_arrive()
    f2, f3 = l2[5], l3[5]
    spread(gf, f2)

    level2.scale()
    level2.sweep(level2.g, level2.u)
    pair2(level2.residual, f3)

    level3.scale()
    m3[0] = jnp.zeros(level3.shape, jnp.float32)
    m3[wide3 - 1] = jnp.zeros(level3.shape, jnp.float32)
    level3.sweep(f3, level3.u)
    now, later = level3.u, m3
    for _ in range(COARSE - 2):
        level3.sweep(now, later)
        now, later = later, now

    p_pack = matrix(
        (LANES, LANES), lambda k, z: (z // half == k // half) & ((z % half) // 2 == k % half), 1.0
    )
    count3, rows3 = wide3 - 2, l3[0].shape[1]
    e3 = dot(now[1 : 1 + count3].reshape(count3 * rows3, LANES), p_pack)
    add_double(tmp, [e3.reshape(count3, rows3, LANES)], level2.u, PAD2, level2.size)
    zero2 = jnp.zeros((PAD2,) + level2.shape, jnp.float32)
    m2[0:PAD2] = zero2
    m2[wide2 - PAD2 :] = zero2
    level2.u[0:PAD2] = zero2
    level2.u[wide2 - PAD2 :] = zero2
    level2.sweep(level2.u, m2)
    level2.sweep(m2, level2.u)

    full = 2 * level2.shape[0]
    shift = lax.rem(full - py * by2, full)
    near = by2 + HY // 2

    halo_u1.arrive()
    halo_u1.unpack(u1, HX1)

    def fetch(c, n):
        e = [level2.u[px * bx2 + c + j] for j in range(n)]
        e = [jnp.concatenate([one, pltpu.roll(one, half, 1)], 0) for one in e]
        e = [pltpu.roll(one, shift, 0) for one in e]
        for j in range(n):
            pe1[c + j, 0:near] = e[j][0:near]
            pe1[c + j, near : near + HY // 2] = e[j][full - HY // 2 : full]

    chunks(0, wide1 // 2, 2 * level2.size, 32, fetch)
    p_one = matrix((LANES, LANES), lambda k, z: z // 2 == k, 1.0)
    e2 = dot(pe1[...].reshape(-1, LANES), p_one).reshape(pe1.shape)
    add_double(tmp, [e2[:, 0 : y1 // 2]], level1.u, 0, level1.size)
    level1.sweep(u1, m1)
    level1.sweep(m1, u1, 1)

    p_zero = matrix((LANES, nz), lambda k, z: z // 2 == k, 1.0)
    base = HX1 - HX0 // 2
    count = wide0 // 2
    e1 = dot(level1.u[base : base + count].reshape(count * y1, LANES), p_zero)
    pe0[...] = e1.reshape(pe0.shape)
    halo_u0.arrive()
    halo_u0.unpack(u0, HX0)
    parts = [pe0[:, 0 : by1 + HY // 2], pe0[:, y1 - HY // 2 : y1]]
    add_double(tmp, parts, level0.u, 0, level0.size)
    level0.sweep(u0, m0, 1)

    def last(x, n):
        v, rest = level0.change(m0, HX0 + x, n)
        den[pl.ds(x, n)] = (0.2 * v + rest)[:, 0:by]

    quarter = bx // OUT_PARTS
    results = []
    for part in range(OUT_PARTS):
        chunks(part * quarter, (part + 1) * quarter, level0.size, 24, last)
        at = pl.ds(part * quarter, quarter)
        results.append(pltpu.make_async_copy(den.at[at], out.at[at], copy_sem.at[part]))
        results[-1].start()

    for h in all_halos:
        h.sent()
    for done in (ma_sent, mb_sent, fa_sent, fb_sent):
        done()
    for copy in results:
        copy.wait()


def per_device(px_count, py_count, source, density):
    bx, by, nz = source.shape
    f32 = jnp.float32
    bx1, by1, bx2, by2 = bx // 2, by // 2, bx // 4, by // 4

    def level(wide, rows, lanes):
        return [pltpu.VMEM((wide, rows, lanes), f32)] * 7

    y0, y1 = by + 2 * HY, by1 + 2 * HY
    wide0, wide1 = bx + 2 * HX0, bx1 + 2 * HX1
    x2, rows2 = bx2 * px_count, by2 * py_count // 2
    ext = pltpu.VMEM(source.shape, f32)

    def halo(hx, pieces, rows, cols, lanes):
        copies = pltpu.SemaphoreType.DMA((2 + sum(6 if c else 2 for _, _, c in pieces),))
        return [
            pltpu.VMEM((2, hx, cols, lanes), f32),
            pltpu.VMEM((2, hx, cols, lanes), f32),
            [pltpu.VMEM((2, rows, w, lanes), f32) for _, w, _ in pieces],
            [pltpu.VMEM((2, rows + 2 * hx, w, lanes), f32) for _, w, _ in pieces],
            copies,
            copies,
        ]

    take = -(-(y1 // 2) // ROWS) * ROWS
    gather = pltpu.VMEM((px_count, py_count, bx2 * by2 // 2, LANES), f32)
    scratch = [
        ext,
        ext,
        level(wide0, y0, nz),
        level(wide1, y1, LANES),
        level(x2 + 2 * PAD2, rows2, LANES),
        level(x2 // 2 + 2, rows2 // 2, LANES),
        pltpu.VMEM((wide0 // 2, y1, nz), f32),
        pltpu.VMEM((wide1 // 2, take, LANES), f32),
        pltpu.VMEM((bx2 * by2, LANES), f32),
        pltpu.VMEM((nz // LANES, max(wide0, wide1, x2) // 2, max(y0, y1, rows2), LANES), f32),
        gather,
        gather,
        pltpu.SemaphoreType.DMA((OUT_PARTS,)),
        [
            halo(3, THREE0, bx, by, nz),
            halo(2, TWO0, bx, by, nz),
            halo(2, TWO0, bx, by, nz),
            halo(3, THREE, bx1, by1, LANES),
            halo(2, TWO, bx1, by1, LANES),
            halo(3, THREE, bx1, by1, LANES),
        ],
        pltpu.SemaphoreType.DMA((2 * (py_count - 1),)),
        pltpu.SemaphoreType.DMA((2 * (py_count - 1),)),
        pltpu.SemaphoreType.DMA((2 * (px_count - 1),)),
        pltpu.SemaphoreType.DMA((2 * (px_count - 1),)),
    ]
    return pl.pallas_call(
        functools.partial(kernel, (px_count, py_count)),
        out_shape=jax.ShapeDtypeStruct(source.shape, f32),
        in_specs=[pl.BlockSpec(memory_space=pl.ANY)] * 2,
        out_specs=pl.BlockSpec(memory_space=pl.ANY),
        scratch_shapes=scratch,
        compiler_params=pltpu.CompilerParams(
            collective_id=0, has_side_effects=True, vmem_limit_bytes=56 * 1024 * 1024
        ),
    )(source, density)


def solution(mesh):
    spec = P("px", "py", None)
    return jax.shard_map(
        functools.partial(per_device, mesh.shape["px"], mesh.shape["py"]),
        mesh=mesh,
        in_specs=(spec, spec),
        out_specs=spec,
        check_vma=False,
    )
```

```python
import functools

import jax
import jax.numpy as jnp
from jax import lax
from jax.experimental import pallas as pl
from jax.experimental.pallas import tpu as pltpu
from jax.sharding import PartitionSpec as P

COARSE = 8
OUT_PARTS = 4
LANES = 128
HX0, HX1, HY, PAD2 = 4, 4, 4, 2
THREE, TWO = ((0, 2, 3), (2, 1, 3)), ((0, 2, 2),)
THREE0, TWO0 = ((0, 2, 2), (2, 1, 0)), ((0, 2, 1),)
ROWS = 8
DIRECTIONS = [(dx, dy) for dx in (-1, 0, 1) for dy in (-1, 0, 1) if (dx, dy) != (0, 0)]
MESH = pl.DeviceIdType.MESH


def iota(shape, dim):
    return lax.broadcasted_iota(jnp.int32, shape, dim)


def dot(a, b):
    total = None
    for _ in range(3):
        part = a.astype(jnp.bfloat16)
        a = a - part.astype(jnp.float32)
        term = jnp.dot(part, b, preferred_element_type=jnp.float32)
        total = term if total is None else total + term
    return total


def matrix(shape, test, value):
    chosen = jnp.where(test(iota(shape, 0), iota(shape, 1)), value, 0.0)
    return chosen.astype(jnp.bfloat16)


def loop(low, high, body, unroll=1):
    def step(i, carry):
        body(i)
        return carry

    lax.fori_loop(low, high, step, 0, unroll=unroll)


def chunks(low, high, size, most, body):
    count = high - low
    n = max(d for d in range(1, count + 1) if count % d == 0 and (d == 1 or d * size <= most))
    if n == count:
        body(low, n)
    else:
        loop(0, count // n, lambda i: body(low + i * n, n))


class Level:
    def __init__(self, refs, factor, start, total, rows, lanes, span, packed):
        (self.m, self.wx, self.wy, self.wz, self.k, self.g, self.u) = refs
        self.low, self.high = span
        self.half = 0.5 * factor
        self.start, self.total = start, total
        shape = self.m.shape[1:]
        self.shape, self.packed = shape, packed
        row, lane = iota(shape, 0), iota(shape, 1)
        first, total_y = rows
        nz, stride = lanes
        group = lane // stride if packed else 0
        gy = row + group * shape[0]
        if not packed:
            gy = first + jnp.where(row < shape[0] - HY, row, row - shape[0])
        gz = lane % stride if packed else lane
        self.row = row
        self.size = -(-shape[0] // ROWS) * (shape[1] // LANES)

        def keep(pos, count, span):
            plus = (pos != count - 1) & (pos != -1) & (pos != span - 1)
            minus = (pos != 0) & (pos != count)
            return jnp.where(plus, 1.0, 0.0), jnp.where(minus, 1.0, 0.0)

        self.kyp, self.kym = keep(gy, total_y, -9)
        self.kzp, self.kzm = keep(gz, nz, stride)
        self.gz, self.nz = gz, nz

    def y_minus(self, t):
        r = pltpu.roll(t, 1, t.ndim - 2)
        if self.packed:
            r = jnp.where(self.row == 0, pltpu.roll(r, LANES // 2, r.ndim - 1), r)
        return r

    def y_plus(self, t):
        r = pltpu.roll(t, self.shape[0] - 1, t.ndim - 2)
        if self.packed:
            r = jnp.where(self.row == self.shape[0] - 1, pltpu.roll(r, LANES // 2, r.ndim - 1), r)
        return r

    def z_minus(self, t):
        return pltpu.roll(t, 1, t.ndim - 1)

    def z_plus(self, t):
        return pltpu.roll(t, self.shape[1] - 1, t.ndim - 1)

    def clear(self, *refs):
        for i in (self.low - 1, self.high):
            for ref in refs:
                ref[i] = jnp.zeros(self.shape, jnp.float32)

    def face(self, x):
        gx = self.start + x
        return jnp.where((gx != self.total - 1) & (gx != -1), 1.0, 0.0)

    def setup(self, source=None):
        before = self.low - 1
        self.wx[before] = (self.half * self.face(before)) * (self.m[before] + self.m[self.low])
        known = self.kyp + self.kym + self.kzp + self.kzm

        def body(x, n):
            m = [self.m[x - 1 + j] for j in range(n + 2)]
            f = None if source is None else [source(x + j) for j in range(n)]
            k = [self.face(x - 1 + j) for j in range(n + 1)]
            s = [k[j] * (m[j] + m[j + 1]) for j in range(n + 1)]
            done = []
            for j in range(n):
                c = m[j + 1]
                wyp = self.kyp * (c + self.y_plus(c))
                wym = self.kym * (c + self.y_minus(c))
                wzp = self.kzp * (c + self.z_plus(c))
                wzm = self.kzm * (c + self.z_minus(c))
                missing = 6.0 - (k[j] + k[j + 1]) - known
                diag = ((s[j] + s[j + 1]) + (wyp + wym)) + ((wzp + wzm) + 2.0 * c * missing)
                done.append((self.half * s[j + 1], self.half * wyp, self.half * wzp,
                             0.8 / (self.half * diag)))
            for j, (wx, wy, wz, inverse) in enumerate(done):
                self.wx[x + j] = wx
                self.wy[x + j] = wy
                self.wz[x + j] = wz
                self.k[x + j] = inverse
                if f is not None:
                    self.g[x + j] = inverse * f[j]

        chunks(self.low, self.high, self.size, 12, body)

    def scale(self):
        def body(x, n):
            at = pl.ds(x, n)
            self.g[at] = self.k[at] * self.g[at]

        chunks(self.low, self.high, self.size, 24, body)

    def change(self, ref, x, n):
        at = pl.ds(x, n)
        wide, wx = ref[pl.ds(x - 1, n + 2)], self.wx[pl.ds(x - 1, n + 1)]
        v, wy, wz = wide[1 : n + 1], self.wy[at], self.wz[at]
        total = wx[1 : n + 1] * wide[2 : n + 2] + wx[0:n] * wide[0:n]
        total = total + (wy * self.y_plus(v) + self.y_minus(wy * v))
        total = total + (wz * self.z_plus(v) + self.z_minus(wz * v))
        return v, self.g[at] + self.k[at] * total

    def sweep(self, src, dst, inset=0):
        def body(x, n):
            v, rest = self.change(src, x, n)
            dst[pl.ds(x, n)] = 0.2 * v + rest

        chunks(self.low + inset, self.high - inset, self.size, 24, body)

    def residual(self, x, n):
        v, rest = self.change(self.u, x, n)
        return (rest - 0.8 * v) / self.k[pl.ds(x, n)]


def columns(width):
    return [slice(c, c + LANES) for c in range(0, width, LANES)]


def pair_slabs(tmp, i, value):
    count, rows, width = value.shape
    sums = [value[j] + value[j + 1] for j in range(0, count, 2)]
    for j, both in enumerate(sums):
        for k, c in enumerate(columns(width)):
            tmp[k, i + j, 0:rows] = both[:, c]


def pair_rows(tmp, count, rows, width):
    parts = [
        tmp[k, 0:count, pl.ds(0, rows, stride=2)] + tmp[k, 0:count, pl.ds(1, rows, stride=2)]
        for k in range(width // LANES)
    ]
    return parts[0] if len(parts) == 1 else jnp.concatenate(parts, 2)


def add_double(tmp, values, target, first, size):
    rows = 0
    for value in values:
        count, more, width = value.shape
        for k, c in enumerate(columns(width)):
            tmp[k, 0:count, pl.ds(2 * rows, more, stride=2)] = value[:, :, c]
            tmp[k, 0:count, pl.ds(2 * rows + 1, more, stride=2)] = value[:, :, c]
        rows += more

    def body(i, n):
        parts = [tmp[k, pl.ds(i, n), 0 : 2 * rows] for k in range(width // LANES)]
        e = parts[0] if len(parts) == 1 else jnp.concatenate(parts, 2)
        old = target[pl.ds(first + 2 * i, 2 * n)]
        new = [old[j] + e[j // 2] for j in range(2 * n)]
        for j in range(2 * n):
            target[first + 2 * i + j] = new[j]

    chunks(0, count, 2 * size, 24, body)


def kernel(sizes, source, density, out, den, src, l0, l1, l2, l3, pe0, pe1, t1, tmp,
           gm, gf, copy_sem, halos, sa, ra, sb, rb):
    px_count, py_count = sizes
    px, py = lax.axis_index("px"), lax.axis_index("py")
    bx, by, nz = source.shape
    nx, ny = bx * px_count, by * py_count
    bx1, by1, bx2, by2 = bx // 2, by // 2, bx // 4, by // 4

    def inside(dx, dy):
        test = None
        for d, pos, count in ((dx, px, px_count), (dy, py, py_count)):
            if d:
                one = (pos < count - 1) if d > 0 else (pos > 0)
                test = one if test is None else test & one
        return test

    class Halo:
        def __init__(self, refs, hx, pieces, block):
            self.xsend, self.xland, self.ysend, self.yland, self.send, self.recv = refs
            self.hx, self.pieces, self.block = hx, pieces, block

        def fill(self, value):
            edges = ((px == 0, 0, 0), (px == px_count - 1, 0, 1),
                     (py == 0, 1, 0), (py == py_count - 1, 1, 1))
            hx, bx = self.hx, self.block[0]
            for test, dim, side in edges:
                @pl.when(test)
                def _():
                    if dim == 0:
                        ref = self.xland
                        ref[side] = jnp.full(ref.shape[1:], value, jnp.float32)
                    for ref in self.yland:
                        if dim:
                            ref[side] = jnp.full(ref.shape[1:], value, jnp.float32)
                        else:
                            at = side * (hx + bx)
                            for s in range(2):
                                ref[s, at : at + hx] = jnp.full((hx,) + ref.shape[2:], value, jnp.float32)

        def pack(self, ref, ox):
            hx, (bx, by) = self.hx, self.block
            self.xsend[0] = ref[ox : ox + hx, 0:by]
            self.xsend[1] = ref[ox + bx - hx : ox + bx, 0:by]
            for ysend, (d, w, _) in zip(self.ysend, self.pieces):
                ysend[0] = ref[ox : ox + bx, d : d + w]
                ysend[1] = ref[ox : ox + bx, by - d - w : by - d]

        def each(self, act, sign):
            hx, bx = self.hx, self.block[0]
            n = 0
            for dx, dy in DIRECTIONS:
                if dy == 0:
                    side = (dx + 1) // 2
                    pairs = [(self.xsend.at[side], self.xland.at[1 - side])]
                else:
                    side = (dy + 1) // 2
                    pairs = []
                    for a, b, (_, _, corner) in zip(self.ysend, self.yland, self.pieces):
                        own, there, count = (
                            (0, hx + bx, corner), (0, hx, bx), (bx - corner, hx - corner, corner)
                        )[dx + 1]
                        if count:
                            pairs.append(
                                (a.at[side, pl.ds(own, count)], b.at[1 - side, pl.ds(there, count)])
                            )
                copies = []
                for a, b in pairs:
                    copies.append(pltpu.make_async_remote_copy(
                        src_ref=a,
                        dst_ref=b,
                        send_sem=self.send.at[n],
                        recv_sem=self.recv.at[n],
                        device_id=(px + dx, py + dy),
                        device_id_type=MESH,
                    ))
                    n += 1

                @pl.when(inside(sign * dx, sign * dy))
                def _():
                    for copy in copies:
                        act(copy)

        def start(self):
            self.each(lambda c: c.start(), 1)

        def arrive(self):
            self.each(lambda c: c.wait_recv(), -1)

        def sent(self):
            self.each(lambda c: c.wait_send(), 1)

        def unpack(self, ref, ox, change=lambda v: v):
            hx, (bx, by), rows = self.hx, self.block, ref.shape[1]
            ref[ox - hx : ox, 0:by] = change(self.xland[0])
            ref[ox + bx : ox + bx + hx, 0:by] = change(self.xland[1])
            for yland, (d, w, _) in zip(self.yland, self.pieces):
                ref[ox - hx : ox + bx + hx, rows - d - w : rows - d] = change(yland[0])
                ref[ox - hx : ox + bx + hx, by + d : by + d + w] = change(yland[1])

    def along(axis, ref, send, recv, base):
        count, me = (py_count, py) if axis else (px_count, px)
        region = ref.at[px, py] if axis else ref.at[px]

        def each(act):
            for k in range(1, count):
                to = lax.rem(me + k, count)
                act(pltpu.make_async_remote_copy(
                    src_ref=region,
                    dst_ref=region,
                    send_sem=send.at[base + k - 1],
                    recv_sem=recv.at[base + k - 1],
                    device_id=(px, to) if axis else (to, py),
                    device_id_type=MESH,
                ))

        def arrive(steps=range(1, count)):
            for k in steps:
                frm = lax.rem(me + count - k, count)
                landed = ref.at[px, frm] if axis else ref.at[frm]
                pltpu.make_async_remote_copy(
                    src_ref=landed,
                    dst_ref=landed,
                    send_sem=send.at[base + k - 1],
                    recv_sem=recv.at[base + k - 1],
                    device_id=(px, frm) if axis else (frm, py),
                    device_id_type=MESH,
                ).wait_recv()

        return (lambda: each(lambda c: c.start())), arrive, (lambda: each(lambda c: c.wait_send()))

    m0, f0, u0 = l0[0], l0[5], l0[6]
    m1, f1, u1 = l1[0], l1[5], l1[6]
    own_copies = [
        pltpu.make_async_copy(a, b, copy_sem.at[i])
        for i, (a, b) in enumerate(((density, den), (source, src)))
    ]
    for c in own_copies:
        c.start()
    block0, block1 = (bx, by), (bx1, by1)
    halo_m0 = Halo(halos[0], 3, THREE0, block0)
    halo_f0 = Halo(halos[1], 2, TWO0, block0)
    halo_u0 = Halo(halos[2], 2, TWO0, block0)
    halo_m1 = Halo(halos[3], 3, THREE, block1)
    halo_f1 = Halo(halos[4], 2, TWO, block1)
    halo_u1 = Halo(halos[5], 3, THREE, block1)
    all_halos = (halo_m0, halo_f0, halo_u0, halo_m1, halo_f1, halo_u1)
    for h, value in zip(all_halos, (1.0, 0.0, 0.0, 1.0, 0.0, 0.0)):
        h.fill(value)

    barrier = pltpu.get_barrier_semaphore()
    for k in range(1, py_count):
        pl.semaphore_signal(barrier, 1, device_id=(px, lax.rem(py + k, py_count)), device_id_type=MESH)
    for k in range(1, px_count):
        pl.semaphore_signal(barrier, 1, device_id=(lax.rem(px + k, px_count), py), device_id_type=MESH)
    for dx, dy in DIRECTIONS:
        if dx and dy:
            @pl.when(inside(dx, dy))
            def _():
                pl.semaphore_signal(barrier, 1, device_id=(px + dx, py + dy), device_id_type=MESH)
    beside_x = jnp.minimum(px, 1) + jnp.minimum(px_count - 1 - px, 1)
    beside_y = jnp.minimum(py, 1) + jnp.minimum(py_count - 1 - py, 1)
    own_copies[0].wait()
    halo_m0.pack(den, 0)
    pl.semaphore_wait(barrier, px_count + py_count - 2 + beside_x * beside_y)

    halo_m0.start()
    own_copies[1].wait()
    halo_f0.pack(src, 0)
    halo_f0.start()

    r_fine = matrix((nz, LANES), lambda z, c: z // 2 == c, 0.125)
    r_low = matrix((LANES, LANES), lambda z, c: z // 2 == c, 0.125)
    r_high = matrix((LANES, LANES), lambda z, c: z // 2 + LANES // 2 == c, 0.125)
    half = LANES // 2
    r_pack = matrix(
        (LANES, LANES), lambda z, c: (z // half == c // half) & ((z % half) // 2 == c % half), 0.125
    )

    def restrict0(get, dst):
        def body(i, n):
            pair_slabs(tmp, i, get(HX0 + 2 * i, 2 * n))

        chunks(0, bx1, 2 * (y0 // ROWS) * (nz // LANES), 24, body)
        value = dot(pair_rows(tmp, bx1, by1, nz).reshape(bx1 * by1, nz), r_fine)
        dst[HX1 : HX1 + bx1, 0:by1] = value.reshape(bx1, by1, LANES)

    def restrict1(get, dst):
        def body(i, n):
            pair_slabs(tmp, i, get(HX1 + 2 * i, 2 * n))

        chunks(0, bx2, 2 * (y1 // ROWS), 24, body)
        sums = pair_rows(tmp, bx2, by2, LANES)
        for i in range(bx2):
            t1[i * by2 : (i + 1) * by2] = sums[i]
        n = bx2 * by2 // 2
        dst[px, py] = dot(t1[0:n], r_low) + dot(t1[n : 2 * n], r_high)

    wide0, wide1, wide2, wide3 = (l[0].shape[0] for l in (l0, l1, l2, l3))
    y0, y1 = l0[0].shape[1], l1[0].shape[1]

    def own(x, n):
        m0[pl.ds(HX0 + x, n), 0:by] = 1.0 / den[pl.ds(x, n)]
        f0[pl.ds(HX0 + x, n), 0:by] = src[pl.ds(x, n)]

    chunks(0, bx, (by // ROWS) * (nz // LANES), 24, own)
    restrict0(lambda x, n: m0[pl.ds(x, n), 0:by], m1)
    halo_m1.pack(m1, HX1)
    halo_m1.start()
    restrict1(lambda x, n: m1[pl.ds(x, n), 0:by1], gm)
    ma_start, ma_arrive, ma_sent = along(1, gm, sa, ra, 0)
    fa_start, fa_arrive, fa_sent = along(1, gf, sa, ra, py_count - 1)
    mb_start, mb_arrive, mb_sent = along(0, gm, sb, rb, 0)
    _, fb_arrive, fb_sent = along(0, gf, sb, rb, px_count - 1)
    ma_start()

    def forward(k):
        block = gf.at[px, lax.rem(py + py_count - k, py_count)]
        for step in range(1, px_count):
            pltpu.make_async_remote_copy(
                src_ref=block,
                dst_ref=block,
                send_sem=sb.at[px_count - 1 + step - 1],
                recv_sem=rb.at[px_count - 1 + step - 1],
                device_id=(lax.rem(px + step, px_count), py),
                device_id_type=MESH,
            ).start()

    level0 = Level(l0, 1.0, px * bx - HX0, nx, (py * by, ny), (nz, nz), (HX0 - 2, HX0 + bx + 2), False)
    level1 = Level(l1, 0.25, px * bx1 - HX1, nx // 2, (py * by1, ny // 2),
                   (nz // 2, LANES), (HX1 - 2, HX1 + bx1 + 2), False)
    level2 = Level(l2, 0.25**2, -PAD2, nx // 4, (0, ny // 4), (nz // 4, half),
                   (PAD2, wide2 - PAD2), True)
    level3 = Level(l3, 0.25**3, -1, nx // 8, (0, ny // 8), (nz // 8, half), (1, wide3 - 1), True)
    level2.clear(level2.g, level2.u)
    level3.clear(level3.g, level3.u)

    def spread(gathered, dst):
        n = bx2 // 2
        lane = iota((n * by2, LANES), 1)
        groups = py_count // 2

        def body(p):
            for q in range(groups):
                a, b = gathered[p, q], gathered[p, q + groups]
                first = jnp.where(lane < half, a, pltpu.roll(b, half, 1))
                second = jnp.where(lane < half, pltpu.roll(a, half, 1), b)
                for i in range(n):
                    rows = slice(q * by2, (q + 1) * by2)
                    piece = slice(i * by2, (i + 1) * by2)
                    dst[PAD2 + p * bx2 + i, rows] = first[piece]
                    dst[PAD2 + p * bx2 + n + i, rows] = second[piece]

        loop(0, px_count, body)

    def pair2(get, dst):
        count = wide3 - 2
        rows = l3[0].shape[1]

        def body(i, n):
            pair_slabs(tmp, i, get(PAD2 + 2 * i, 2 * n))

        chunks(0, count, 2 * level2.size, 24, body)
        sums = pair_rows(tmp, count, rows, LANES)
        dst[1 : 1 + count] = dot(sums.reshape(count * rows, LANES), r_pack).reshape(
            count, rows, LANES
        )

    halo_m0.arrive()
    halo_m0.unpack(m0, HX0, lambda v: 1.0 / v)
    level0.setup()
    halo_f0.arrive()
    halo_f0.unpack(f0, HX0)
    ma_arrive()
    mb_start()
    level0.scale()
    level0.sweep(f0, u0, 1)
    restrict0(lambda x, n: level0.residual(x, n)[:, 0:by], f1)
    halo_f1.pack(f1, HX1)
    halo_f1.start()
    halo_u0.pack(u0, HX0)

    halo_m1.arrive()
    halo_m1.unpack(m1, HX1)
    level1.setup()
    mb_arrive()
    one2 = jnp.ones((PAD2,) + level2.shape, jnp.float32)
    one3 = jnp.ones(level3.shape, jnp.float32)
    m2, m3 = l2[0], l3[0]
    spread(gm, m2)
    m2[0:PAD2] = one2
    m2[wide2 - PAD2 :] = one2
    level2.setup()
    halo_f1.arrive()
    halo_f1.unpack(f1, HX1)
    level1.scale()
    level1.sweep(f1, u1, 1)
    restrict1(lambda x, n: level1.residual(x, n)[:, 0:by1], gf)
    fa_start()
    forward(0)
    halo_u1.pack(u1, HX1)
    pair2(lambda x, n: m2[pl.ds(x, n)], m3)
    m3[0] = one3
    m3[wide3 - 1] = one3

    inner3 = slice(1, wide3 - 1)
    m3[inner3] = jnp.where(level3.gz < level3.nz, m3[inner3], 1.0)
    level3.setup()


    for k in sorted(range(1, py_count), key=lambda k: (min(k, py_count - k), k)):
        fa_arrive([k])
        forward(k)
    halo_u1.start()
    halo_u0.start()
    fb_arrive()
    f2, f3 = l2[5], l3[5]
    spread(gf, f2)

    level2.scale()
    level2.sweep(level2.g, level2.u)
    pair2(level2.residual, f3)

    level3.scale()
    m3[0] = jnp.zeros(level3.shape, jnp.float32)
    m3[wide3 - 1] = jnp.zeros(level3.shape, jnp.float32)
    level3.sweep(f3, level3.u)
    now, later = level3.u, m3
    for _ in range(COARSE - 2):
        level3.sweep(now, later)
        now, later = later, now

    p_pack = matrix(
        (LANES, LANES), lambda k, z: (z // half == k // half) & ((z % half) // 2 == k % half), 1.0
    )
    count3, rows3 = wide3 - 2, l3[0].shape[1]
    e3 = dot(now[1 : 1 + count3].reshape(count3 * rows3, LANES), p_pack)
    add_double(tmp, [e3.reshape(count3, rows3, LANES)], level2.u, PAD2, level2.size)
    zero2 = jnp.zeros((PAD2,) + level2.shape, jnp.float32)
    m2[0:PAD2] = zero2
    m2[wide2 - PAD2 :] = zero2
    level2.u[0:PAD2] = zero2
    level2.u[wide2 - PAD2 :] = zero2
    level2.sweep(level2.u, m2)
    level2.sweep(m2, level2.u)

    full = 2 * level2.shape[0]
    shift = lax.rem(full - py * by2, full)
    near = by2 + HY // 2

    halo_u1.arrive()
    halo_u1.unpack(u1, HX1)

    def fetch(c, n):
        e = [level2.u[px * bx2 + c + j] for j in range(n)]
        e = [jnp.concatenate([one, pltpu.roll(one, half, 1)], 0) for one in e]
        e = [pltpu.roll(one, shift, 0) for one in e]
        for j in range(n):
            pe1[c + j, 0:near] = e[j][0:near]
            pe1[c + j, near : near + HY // 2] = e[j][full - HY // 2 : full]

    chunks(0, wide1 // 2, 2 * level2.size, 32, fetch)
    p_one = matrix((LANES, LANES), lambda k, z: z // 2 == k, 1.0)
    e2 = dot(pe1[...].reshape(-1, LANES), p_one).reshape(pe1.shape)
    add_double(tmp, [e2[:, 0 : y1 // 2]], level1.u, 0, level1.size)
    level1.sweep(u1, m1)
    level1.sweep(m1, u1, 1)

    p_zero = matrix((LANES, nz), lambda k, z: z // 2 == k, 1.0)
    base = HX1 - HX0 // 2
    count = wide0 // 2
    e1 = dot(level1.u[base : base + count].reshape(count * y1, LANES), p_zero)
    pe0[...] = e1.reshape(pe0.shape)
    halo_u0.arrive()
    halo_u0.unpack(u0, HX0)
    parts = [pe0[:, 0 : by1 + HY // 2], pe0[:, y1 - HY // 2 : y1]]
    add_double(tmp, parts, level0.u, 0, level0.size)
    level0.sweep(u0, m0, 1)

    def last(x, n):
        v, rest = level0.change(m0, HX0 + x, n)
        den[pl.ds(x, n)] = (0.2 * v + rest)[:, 0:by]

    quarter = bx // OUT_PARTS
    results = []
    for part in range(OUT_PARTS):
        chunks(part * quarter, (part + 1) * quarter, level0.size, 24, last)
        at = pl.ds(part * quarter, quarter)
        results.append(pltpu.make_async_copy(den.at[at], out.at[at], copy_sem.at[part]))
        results[-1].start()

    for h in all_halos:
        h.sent()
    for done in (ma_sent, mb_sent, fa_sent, fb_sent):
        done()
    for copy in results:
        copy.wait()


def per_device(px_count, py_count, source, density):
    bx, by, nz = source.shape
    f32 = jnp.float32
    bx1, by1, bx2, by2 = bx // 2, by // 2, bx // 4, by // 4

    def level(wide, rows, lanes):
        return [pltpu.VMEM((wide, rows, lanes), f32)] * 7

    y0, y1 = by + 2 * HY, by1 + 2 * HY
    wide0, wide1 = bx + 2 * HX0, bx1 + 2 * HX1
    x2, rows2 = bx2 * px_count, by2 * py_count // 2
    ext = pltpu.VMEM(source.shape, f32)

    def halo(hx, pieces, rows, cols, lanes):
        copies = pltpu.SemaphoreType.DMA((2 + sum(6 if c else 2 for _, _, c in pieces),))
        return [
            pltpu.VMEM((2, hx, cols, lanes), f32),
            pltpu.VMEM((2, hx, cols, lanes), f32),
            [pltpu.VMEM((2, rows, w, lanes), f32) for _, w, _ in pieces],
            [pltpu.VMEM((2, rows + 2 * hx, w, lanes), f32) for _, w, _ in pieces],
            copies,
            copies,
        ]

    take = -(-(y1 // 2) // ROWS) * ROWS
    gather = pltpu.VMEM((px_count, py_count, bx2 * by2 // 2, LANES), f32)
    scratch = [
        ext,
        ext,
        level(wide0, y0, nz),
        level(wide1, y1, LANES),
        level(x2 + 2 * PAD2, rows2, LANES),
        level(x2 // 2 + 2, rows2 // 2, LANES),
        pltpu.VMEM((wide0 // 2, y1, nz), f32),
        pltpu.VMEM((wide1 // 2, take, LANES), f32),
        pltpu.VMEM((bx2 * by2, LANES), f32),
        pltpu.VMEM((nz // LANES, max(wide0, wide1, x2) // 2, max(y0, y1, rows2), LANES), f32),
        gather,
        gather,
        pltpu.SemaphoreType.DMA((OUT_PARTS,)),
        [
            halo(3, THREE0, bx, by, nz),
            halo(2, TWO0, bx, by, nz),
            halo(2, TWO0, bx, by, nz),
            halo(3, THREE, bx1, by1, LANES),
            halo(2, TWO, bx1, by1, LANES),
            halo(3, THREE, bx1, by1, LANES),
        ],
        pltpu.SemaphoreType.DMA((2 * (py_count - 1),)),
        pltpu.SemaphoreType.DMA((2 * (py_count - 1),)),
        pltpu.SemaphoreType.DMA((2 * (px_count - 1),)),
        pltpu.SemaphoreType.DMA((2 * (px_count - 1),)),
    ]
    return pl.pallas_call(
        functools.partial(kernel, (px_count, py_count)),
        out_shape=jax.ShapeDtypeStruct(source.shape, f32),
        in_specs=[pl.BlockSpec(memory_space=pl.ANY)] * 2,
        out_specs=pl.BlockSpec(memory_space=pl.ANY),
        scratch_shapes=scratch,
        compiler_params=pltpu.CompilerParams(
            collective_id=0, has_side_effects=True, vmem_limit_bytes=56 * 1024 * 1024
        ),
    )(source, density)


def solution(mesh):
    spec = P("px", "py", None)
    return jax.shard_map(
        functools.partial(per_device, mesh.shape["px"], mesh.shape["py"]),
        mesh=mesh,
        in_specs=(spec, spec),
        out_specs=spec,
        check_vma=False,
    )
```
